256 devices in a mesh: seq: 64 (over y, z, core), tp: 4 (over x).
Axes of the slice: x: 4, y: 4, z: 8, core: 2. Of those that a mesh axis runs over, the one named last changes fastest.
Arguments:
- queries: bfloat16 [65536, 2048], P('seq', 'tp'), may hold values from -2 to 2
- keys: bfloat16 [65536, 2048], P('seq', 'tp'), may hold values from -2 to 2
- values: bfloat16 [65536, 2048], P('seq', 'tp'), may hold values from -16 to 16
- out_grad: bfloat16 [65536, 2048], P('seq', 'tp'), may hold values from -1.5 to 1.5
- gain: float32 [2048], P('tp'), may hold values from 0.25 to 1.75
Outputs:
- query_grad: bfloat16 [65536, 2048], P('seq', 'tp')
- key_grad: bfloat16 [65536, 2048], P('seq', 'tp')
- value_grad: bfloat16 [65536, 2048], P('seq', 'tp')
- gain_grad: float32 [2048], P('tp')
The draws below stay inside these ranges and needn't reach their ends.
All inputs are finite; a program needn't handle non-finite values.
Results may differ from the reference program's by a relative error of at most 0.006.
Values sent between devices are 32-bit elements; how exact they have to be, the bound alone decides.
A program may use at most 128 MiB of HBM per device.

```python
import jax
import jax.numpy as jnp
from jax import lax

HEADS = 16
HEAD_DIM = 128
BLK = 512
TOKENS = 65536


def draw_values(key, part):
    key = jax.random.fold_in(key, 11)
    head_of = jnp.arange(HEADS * HEAD_DIM) // HEAD_DIM
    ramp = head_of.astype(jnp.float32) / max(HEADS - 1, 1)
    base = jnp.clip(jax.random.normal(key, (TOKENS, HEADS * HEAD_DIM), jnp.float32), -4.0, 4.0)
    factor = 3.0 ** ramp
    return (base * factor[None, :]).astype(jnp.bfloat16)


def block_levels(key, extent, pieces, low, largest):
    def one(position, blocks):
        steps = jax.random.uniform(jax.random.fold_in(jax.random.fold_in(key, 6), position), (blocks,), jnp.float32, low / len(pieces), largest / len(pieces))
        return jnp.repeat(jnp.exp(steps), extent[position] // blocks).reshape((-1,) + (1,) * (len(extent) - position - 1))

    level = one(*pieces[0])
    for cut in pieces[1:]:
        level = level * one(*cut)
    return level


def gaussian(own_key, dims, spread, limit, split=(), kind=jnp.bfloat16):
    entries = jax.random.normal(own_key, dims, jnp.float32) * spread
    if len(split) > 0:
        entries = block_levels(own_key, dims, split, -0.22, 0.18) * entries
    return jnp.clip(entries, min=-limit, max=limit).astype(kind)


def setup_inputs(seed: int = 0) -> dict:
    streams_of = jax.random.split(jax.random.key(seed), 6)
    queries = gaussian(streams_of[0], (TOKENS, HEADS * HEAD_DIM), 0.3, 2.0, ((0, 64), (1, 4)))
    keys = gaussian(streams_of[1], (TOKENS, HEADS * HEAD_DIM), 0.3, 2.0, ((0, 64), (1, 4)))
    values = draw_values(jax.random.fold_in(streams_of[5], 71), 0)
    out_grad = gaussian(streams_of[3], (TOKENS, HEADS * HEAD_DIM), 0.2, 1.5, ((0, 64), (1, 4)))
    gain = jnp.clip(1.0 + 0.15 * jax.random.normal(streams_of[4], (HEADS * HEAD_DIM,), jnp.float32), 0.25, 1.75)
    return dict(queries=queries, keys=keys, values=values, out_grad=out_grad, gain=gain)


epsilon = 1e-05

def rounded(array):
    return lax.optimization_barrier(array.astype(jnp.bfloat16)).astype(jnp.float32)

def block_view(array):
    return array.reshape(TOKENS // BLK, BLK, HEADS, HEAD_DIM)

def reference(queries, keys, values, out_grad, gain):
    query_blocks = block_view(queries)
    key_blocks = block_view(keys)
    value_blocks = block_view(values)
    causal = jnp.tril(jnp.ones((BLK, BLK), jnp.bool_))

    def scores_of(query_now, key_now):
        raw_scores = jnp.einsum('thd,shd->hts', query_now.astype(jnp.float32), key_now.astype(jnp.float32))
        return rounded(jnp.where(causal[None], raw_scores, 0.0))

    def forward(running, block):
        query_now, key_now, value_now = block
        prefix = rounded(running)
        scores = scores_of(query_now, key_now)
        attended = jnp.einsum('thd,hde->the', query_now.astype(jnp.float32), prefix)
        attended = attended + jnp.einsum('hts,she->the', scores, value_now.astype(jnp.float32))
        running = running + jnp.einsum('thd,the->hde', key_now.astype(jnp.float32), value_now.astype(jnp.float32))
        return (running, (attended, prefix))
    start_state = jnp.zeros((HEADS, HEAD_DIM, HEAD_DIM), jnp.float32)
    _, (attended, prefixes) = lax.scan(forward, start_state, (query_blocks, key_blocks, value_blocks))
    attended = attended.reshape(TOKENS, HEADS * HEAD_DIM)
    grad_out = out_grad.astype(jnp.float32)
    scaled = gain.astype(jnp.float32)[None, :] * grad_out
    inverse = lax.rsqrt(lax.optimization_barrier(jnp.mean(attended * attended, axis=1, keepdims=True)) + epsilon)
    inner_sum = lax.optimization_barrier(jnp.mean(scaled * attended, axis=1, keepdims=True))
    attn_grad = rounded(inverse * scaled - attended * inverse * inverse * inverse * inner_sum)
    gain_grad = lax.optimization_barrier(jnp.sum(grad_out * attended * inverse, axis=0))
    grad_blocks = block_view(attn_grad)

    def backward(running, block):
        query_now, key_now, value_now, grad_now, prefix = block
        query_now = query_now.astype(jnp.float32)
        key_now = key_now.astype(jnp.float32)
        value_now = value_now.astype(jnp.float32)
        suffix = rounded(running)
        scores = scores_of(query_now, key_now)
        mixing = rounded(jnp.where(causal[None], jnp.einsum('the,she->hts', grad_now, value_now), 0.0))
        query_part = jnp.einsum('the,hde->thd', grad_now, prefix) + jnp.einsum('hts,shd->thd', mixing, key_now)
        key_part = jnp.einsum('the,hde->thd', value_now, suffix) + jnp.einsum('hts,thd->shd', mixing, query_now)
        value_part = jnp.einsum('thd,hde->the', key_now, suffix) + jnp.einsum('hts,the->she', scores, grad_now)
        running = running + jnp.einsum('thd,the->hde', query_now, grad_now)
        return (running, (query_part, key_part, value_part))
    _, (query_grad, key_grad, value_grad) = lax.scan(backward, start_state, (query_blocks, key_blocks, value_blocks, grad_blocks, prefixes), reverse=True)
    shape_out = (TOKENS, HEADS * HEAD_DIM)
    return (query_grad.reshape(shape_out).astype(jnp.bfloat16), key_grad.reshape(shape_out).astype(jnp.bfloat16), value_grad.reshape(shape_out).astype(jnp.bfloat16), gain_grad)
```

```python
import jax
import jax.numpy as jnp
from jax import lax
from jax.experimental import pallas as pl
from jax.experimental.pallas import tpu as pltpu
from jax.sharding import PartitionSpec as P

HEAD_DIM = 128
BLK = 512
HALF = 256
NH = 4
TOK = 1024
FEAT = 512
FULL = 2048.0
YS = 4
ZS = 8
CHIPS = YS * ZS
PIECE = 8
EPS = 1e-05
MESH = pl.DeviceIdType.MESH
F32 = jnp.float32
BF16 = jnp.bfloat16

FIRST_SPLIT = 5
SECOND_SPLIT = 4


def ring(n, d):
    return min(d, n - d)


OFFSETS = sorted(
    [(dy, dz) for dy in range(YS) for dz in range(ZS) if (dy, dz) != (0, 0)],
    key=lambda o: -(ring(YS, o[0]) + ring(ZS, o[1])),
)


def dot_nn(a, b):
    return lax.dot_general(a, b, (((1,), (0,)), ((), ())), preferred_element_type=F32)


def dot_nt(a, b):
    return lax.dot_general(a, b, (((1,), (1,)), ((), ())), preferred_element_type=F32)


def dot_tn(a, b):
    return lax.dot_general(a, b, (((0,), (0,)), ((), ())), preferred_element_type=F32)


def kernel(
    q_hbm, k_hbm, v_hbm, g_hbm, gain_ref,
    qg_ref, kg_ref, vg_ref, gg_ref,
    q, k, v, g, sc, att, da, kga, vga,
    inside, total, sib, piece, rb1, ob1, rb2, xb, edge, pref,
    tpo, tpr, gacc, gown, gsib, gchip, gz, gzs, gy,
    load_sem, send_sem, recv_sem,
):
    me = lax.axis_index("seq")
    tp = lax.axis_index("tp")
    chip = me // 2
    core = me % 2
    yy = chip // ZS
    zz = chip % ZS
    sibling = (me + 1 - 2 * core, tp)

    def chip_at(dy, dz):
        return (yy + dy) % YS * ZS + (zz + dz) % ZS

    chips = [chip_at(dy, dz) for dy, dz in OFFSETS]
    tps = [(me, (tp + d) % 4) for d in (2, 1, 3)]

    barrier = pltpu.get_barrier_semaphore()
    for c in chips:
        pl.semaphore_signal(barrier, inc=1, device_id=(2 * c + core, tp), device_id_type=MESH)
    for t in tps:
        pl.semaphore_signal(barrier, inc=1, device_id=t, device_id_type=MESH)
    pl.semaphore_signal(barrier, inc=1, device_id=sibling, device_id_type=MESH)

    loads = [
        pltpu.make_async_copy(src, dst, load_sem.at[i])
        for i, (src, dst) in enumerate(((k_hbm, k), (v_hbm, v), (q_hbm, q), (g_hbm, g)))
    ]
    for load in loads:
        load.start()

    def remote(src, dst, index, device):
        return pltpu.make_async_remote_copy(
            src_ref=src, dst_ref=dst, send_sem=send_sem.at[index], recv_sem=recv_sem.at[index],
            device_id=device, device_id_type=MESH,
        )

    def rows(i, n):
        return pl.ds(pl.multiple_of(i * n, n), n)

    row_id = lax.broadcasted_iota(jnp.int32, (HALF, HALF), 0)
    col_id = lax.broadcasted_iota(jnp.int32, (HALF, HALF), 1)
    causal = col_id <= row_id

    def where_at(u):
        b = u // NH
        h = u % NH
        start = pl.multiple_of(b * BLK, BLK)
        return b, h, start, pl.ds(pl.multiple_of(h * HEAD_DIM, HEAD_DIM), HEAD_DIM)

    def states(left, right, scan, inner):
        def body(h, carry):
            cols = pl.ds(pl.multiple_of(h * HEAD_DIM, HEAD_DIM), HEAD_DIM)
            first = dot_tn(left[pl.ds(0, BLK), cols], right[pl.ds(0, BLK), cols])
            second = dot_tn(left[pl.ds(BLK, BLK), cols], right[pl.ds(BLK, BLK), cols])
            inside[scan, rows(h, HEAD_DIM), :] = second if inner == 1 else first
            total[scan, rows(h, HEAD_DIM), :] = first + second
            return carry

        lax.fori_loop(0, NH, body, 0, unroll=True)

    def score_unit(u, carry):
        b, h, start, cols = where_at(u)
        upper, lower, both = pl.ds(start, HALF), pl.ds(start + HALF, HALF), pl.ds(start, BLK)
        top = jnp.where(causal, dot_nt(q[upper, cols], k[upper, cols]), 0.0).astype(BF16)
        low = dot_nt(q[lower, cols], k[upper, cols]).astype(BF16)
        end = jnp.where(causal, dot_nt(q[lower, cols], k[lower, cols]), 0.0).astype(BF16)
        sc[u, pl.ds(0, HALF), pl.ds(0, HALF)] = top
        sc[u, pl.ds(HALF, HALF), pl.ds(0, HALF)] = low
        sc[u, pl.ds(HALF, HALF), pl.ds(HALF, HALF)] = end
        att[upper, cols] = dot_nn(top, v[upper, cols])
        att[lower, cols] = dot_nn(low, v[upper, cols]) + dot_nn(end, v[lower, cols])
        return carry

    def mixing_unit(u, carry):
        b, h, start, cols = where_at(u)
        upper, lower, both = pl.ds(start, HALF), pl.ds(start + HALF, HALF), pl.ds(start, BLK)
        d_up, d_low = da[upper, cols], da[lower, cols]
        top = jnp.where(causal, dot_nt(d_up, v[upper, cols]), 0.0).astype(BF16)
        low = dot_nt(d_low, v[upper, cols]).astype(BF16)
        end = jnp.where(causal, dot_nt(d_low, v[lower, cols]), 0.0).astype(BF16)
        before = pref[b, rows(h, HEAD_DIM), :]
        k_up, k_low = k[upper, cols], k[lower, cols]
        qg_ref[upper, cols] = (dot_nt(d_up, before) + dot_nn(top, k_up)).astype(BF16)
        qg_ref[lower, cols] = (
            dot_nt(d_low, before) + dot_nn(low, k_up) + dot_nn(end, k_low)
        ).astype(BF16)
        q_up, q_low = q[upper, cols], q[lower, cols]
        kga[upper, cols] = dot_tn(top, q_up) + dot_tn(low, q_low)
        kga[lower, cols] = dot_tn(end, q_low)
        s_top = sc[u, pl.ds(0, HALF), pl.ds(0, HALF)]
        s_low = sc[u, pl.ds(HALF, HALF), pl.ds(0, HALF)]
        s_end = sc[u, pl.ds(HALF, HALF), pl.ds(HALF, HALF)]
        vga[upper, cols] = dot_tn(s_top, d_up) + dot_tn(s_low, d_low)
        vga[lower, cols] = dot_tn(s_end, d_low)
        return carry

    mine = rows(core, HALF)
    other = rows(1 - core, HALF)

    def scan_sums(scan, base, work, split, forward, with_gain):
        copies = []
        give = remote(total.at[scan, other], sib.at[scan], base, sibling)
        give.start()
        if with_gain:
            give_gain = remote(gown, gsib, base + 4, sibling)
            give_gain.start()
        give.wait_recv()
        piece[scan] = total[scan, mine, :] + sib[scan]
        for c in chips:
            remote(
                piece.at[scan, rows(c, PIECE)], rb1.at[scan, rows(chip, PIECE)], base + 1, (2 * c + core, tp)
            ).start()
        rb1[scan, rows(chip, PIECE), :] = piece[scan, rows(chip, PIECE), :]
        if with_gain:
            give_gain.wait_recv()
            gchip[...] = gown[...] + gsib[...]
            for d in (4, 3, 5, 2, 6, 1, 7):
                c = chip_at(0, d)
                remote(gchip, gz.at[zz], base + 5, (2 * c + core, tp)).start()
            gz[zz] = gchip[...]
        lax.fori_loop(0, split, work, 0)
        nothing = (CHIPS - 1) * PIECE
        wait1 = remote(piece.at[scan, pl.ds(0, nothing)], rb1.at[scan, pl.ds(0, nothing)], base + 1, sibling)
        wait1.wait_recv()
        running = jnp.zeros((PIECE, HEAD_DIM), F32)
        for i in range(CHIPS):
            at = pl.ds((i if forward else CHIPS - 1 - i) * PIECE, PIECE)
            ob1[scan, at, :] = running
            running = running + rb1[scan, at, :]
        for c in chips:
            remote(
                ob1.at[scan, rows(c, PIECE)], rb2.at[scan, rows(chip, PIECE)], base + 2, (2 * c + core, tp)
            ).start()
        rb2[scan, rows(chip, PIECE), :] = ob1[scan, rows(chip, PIECE), :]
        if with_gain:
            wait_z = remote(gz.at[pl.ds(0, ZS - 1)], gz.at[pl.ds(0, ZS - 1)], base + 5, sibling)
            wait_z.wait_recv()
            gzs[...] = jnp.sum(gz[...], axis=0)
            for d in (2, 1, 3):
                c = chip_at(d, 0)
                remote(gzs, gy.at[yy], base + 6, (2 * c + core, tp)).start()
            gy[yy] = gzs[...]
        lax.fori_loop(split, 2 * NH, work, 0)
        wait2 = remote(ob1.at[scan, pl.ds(0, nothing)], rb2.at[scan, pl.ds(0, nothing)], base + 2, sibling)
        wait2.wait_recv()
        late = core == 1 if forward else core == 0
        arrived = rb2[scan]
        xb[scan] = arrived + jnp.where(late, 0.0, total[scan, mine, :])
        swap = remote(xb.at[scan], edge.at[scan, mine], base + 3, sibling)
        swap.start()
        edge[scan, mine, :] = arrived + jnp.where(late, sib[scan], 0.0)
        swap.wait_recv()
        give.wait_send()
        wait1.wait_send()
        wait2.wait_send()
        swap.wait_send()
        if with_gain:
            give_gain.wait_send()
            wait_z.wait_send()
            wait_y = remote(gy.at[pl.ds(0, YS - 1)], gy.at[pl.ds(0, YS - 1)], base + 6, sibling)
            wait_y.wait_recv()
            wait_y.wait_send()
            gg_ref[...] = jnp.sum(gy[...], axis=0)[:NH]

    loads[0].wait()
    loads[1].wait()
    states(k, v, 0, 0)
    pl.semaphore_wait(barrier, CHIPS - 1 + 3 + 1)
    loads[2].wait()
    scan_sums(0, 0, score_unit, FIRST_SPLIT, True, False)
    loads[3].wait()

    pref[0] = edge[0].astype(BF16)
    pref[1] = (edge[0] + inside[0]).astype(BF16)
    eye = (
        lax.broadcasted_iota(jnp.int32, (HEAD_DIM, HEAD_DIM), 0)
        == lax.broadcasted_iota(jnp.int32, (HEAD_DIM, HEAD_DIM), 1)
    )

    def attend(i, carry):
        b = i // (BLK // HEAD_DIM)
        here = rows(i, HEAD_DIM)
        squares = jnp.zeros((HEAD_DIM, HEAD_DIM), F32)
        inner = jnp.zeros((HEAD_DIM, HEAD_DIM), F32)
        for h in range(NH):
            cols = pl.ds(h * HEAD_DIM, HEAD_DIM)
            a = att[here, cols] + dot_nn(q[here, cols], pref[b, pl.ds(h * HEAD_DIM, HEAD_DIM), :])
            att[here, cols] = a
            squares = squares + a * a
            inner = inner + gain_ref[:, cols] * g[here, cols].astype(F32) * a
        sq = jnp.sum(squares, axis=1, keepdims=True)
        inn = jnp.sum(inner, axis=1, keepdims=True)
        tpo[pl.ds(i, 1), :] = jnp.sum(jnp.where(eye, sq, 0.0), axis=0, keepdims=True)
        tpo[pl.ds(i + 8, 1), :] = jnp.sum(jnp.where(eye, inn, 0.0), axis=0, keepdims=True)
        return carry

    lax.fori_loop(0, TOK // HEAD_DIM, attend, 0, unroll=2)
    sends = [remote(tpo, tpr.at[i], 11 + i, t) for i, t in enumerate(tps)]
    for s in sends:
        s.start()
    for s in sends:
        s.wait_recv()
    sums = tpo[...] + tpr[0] + tpr[1] + tpr[2]
    for s in sends:
        s.wait_send()
    inverse = lax.rsqrt(sums[:8] / FULL + EPS)
    tpo[pl.ds(0, 8), :] = inverse
    tpo[pl.ds(8, 8), :] = inverse * inverse * inverse * (sums[8:] / FULL)
    gacc[...] = jnp.zeros_like(gacc)

    def grads(i, carry):
        here = rows(i, HEAD_DIM)
        r = jnp.sum(jnp.where(eye, tpo[pl.ds(i, 1), :], 0.0), axis=1, keepdims=True)
        m = jnp.sum(jnp.where(eye, tpo[pl.ds(i + 8, 1), :], 0.0), axis=1, keepdims=True)
        for h in range(NH):
            cols = pl.ds(h * HEAD_DIM, HEAD_DIM)
            a = att[here, cols]
            gr = g[here, cols].astype(F32) * r
            da[here, cols] = (gain_ref[:, cols] * gr - a * m).astype(BF16)
            gacc[h] += jnp.sum((gr * a).reshape(HEAD_DIM // 8, 8, HEAD_DIM), axis=0)
        return carry

    lax.fori_loop(0, TOK // HEAD_DIM, grads, 0, unroll=2)
    states(q, da, 1, 1)
    for h in range(NH):
        gown[pl.ds(h, 1), :] = jnp.sum(gacc[h], axis=0, keepdims=True)
        gown[pl.ds(h + NH, 1), :] = jnp.zeros((1, HEAD_DIM), F32)
    scan_sums(1, 4, mixing_unit, SECOND_SPLIT, False, True)

    pref[0] = (edge[1] + inside[1]).astype(BF16)
    pref[1] = edge[1].astype(BF16)

    def finish(u, carry):
        b, h, start, cols = where_at(u)
        both = pl.ds(start, BLK)
        after = pref[b, rows(h, HEAD_DIM), :]
        kg_ref[both, cols] = (dot_nt(v[both, cols], after) + kga[both, cols]).astype(BF16)
        vg_ref[both, cols] = (dot_nn(k[both, cols], after) + vga[both, cols]).astype(BF16)
        return carry

    lax.fori_loop(0, 2 * NH, finish, 0, unroll=2)


def local(queries, keys, values, out_grad, gain):
    vmem = pltpu.VMEM
    big = jax.ShapeDtypeStruct((TOK, FEAT), BF16)
    state = (2, NH * HEAD_DIM, HEAD_DIM)
    half = (2, HALF, HEAD_DIM)
    tile = (8, HEAD_DIM)
    anywhere = pl.BlockSpec(memory_space=pl.ANY)
    whole = pl.BlockSpec(memory_space=vmem)
    out = pl.pallas_call(
        kernel,
        name="attention_backward",
        out_shape=(big, big, big, jax.ShapeDtypeStruct((NH, HEAD_DIM), F32)),
        in_specs=[anywhere] * 4 + [whole],
        out_specs=(whole,) * 4,
        scratch_shapes=[
            vmem((TOK, FEAT), BF16),
            vmem((TOK, FEAT), BF16),
            vmem((TOK, FEAT), BF16),
            vmem((TOK, FEAT), BF16),
            vmem((2 * NH, BLK, BLK), BF16),
            vmem((TOK, FEAT), F32),
            vmem((TOK, FEAT), BF16),
            vmem((TOK, FEAT), F32),
            vmem((TOK, FEAT), F32),
            vmem(state, F32),
            vmem(state, F32),
            vmem(half, F32),
            vmem(half, F32),
            vmem(half, F32),
            vmem(half, F32),
            vmem(half, F32),
            vmem(half, F32),
            vmem(state, F32),
            vmem(state, BF16),
            vmem((16, HEAD_DIM), F32),
            vmem((3, 16, HEAD_DIM), F32),
            vmem((NH, 8, HEAD_DIM), F32),
            vmem(tile, F32),
            vmem(tile, F32),
            vmem(tile, F32),
            vmem((ZS, 8, HEAD_DIM), F32),
            vmem(tile, F32),
            vmem((YS, 8, HEAD_DIM), F32),
            pltpu.SemaphoreType.DMA((4,)),
            pltpu.SemaphoreType.DMA((14,)),
            pltpu.SemaphoreType.DMA((14,)),
        ],
        compiler_params=pltpu.CompilerParams(
            collective_id=0, has_side_effects=True, vmem_limit_bytes=48 * 1024 * 1024
        ),
    )(queries, keys, values, out_grad, gain.reshape(1, FEAT))
    return out[0], out[1], out[2], out[3].reshape(FEAT)


def solution(mesh):
    in_specs = (P("seq", "tp"), P("seq", "tp"), P("seq", "tp"), P("seq", "tp"), P("tp"))
    out_specs = (P("seq", "tp"), P("seq", "tp"), P("seq", "tp"), P("tp"))
    return jax.shard_map(local, mesh=mesh, in_specs=in_specs, out_specs=out_specs, check_vma=False)
```

```python
import jax
import jax.numpy as jnp
from jax import lax
from jax.experimental import pallas as pl
from jax.experimental.pallas import tpu as pltpu
from jax.sharding import PartitionSpec as P

HEAD_DIM = 128
BLK = 512
HALF = 256
NH = 4
TOK = 1024
FEAT = 512
FULL = 2048.0
YS = 4
ZS = 8
CHIPS = YS * ZS
PIECE = 8
EPS = 1e-05
MESH = pl.DeviceIdType.MESH
F32 = jnp.float32
BF16 = jnp.bfloat16

FIRST_SPLIT = 5
SECOND_SPLIT = 4
UNROLL = 8


def ring(n, d):
    return min(d, n - d)


OFFSETS = sorted(
    [(dy, dz) for dy in range(YS) for dz in range(ZS) if (dy, dz) != (0, 0)],
    key=lambda o: -(ring(YS, o[0]) + ring(ZS, o[1])),
)


def dot_nn(a, b):
    return lax.dot_general(a, b, (((1,), (0,)), ((), ())), preferred_element_type=F32)


def dot_nt(a, b):
    return lax.dot_general(a, b, (((1,), (1,)), ((), ())), preferred_element_type=F32)


def dot_tn(a, b):
    return lax.dot_general(a, b, (((0,), (0,)), ((), ())), preferred_element_type=F32)


def kernel(
    q_hbm, k_hbm, v_hbm, g_hbm, gain_hbm,
    qg_ref, kg_ref, vg_ref, gg_ref,
    q, k, v, g, gain, sc, att, scaled, da, kga, vga, rcol, mcol,
    inside, total, sib, piece, rb1, ob1, rb2, xb, edge, pref,
    tpo, tpr, gchip, gz, gzs, gy,
    load_sem, send_sem, recv_sem,
):
    me = lax.axis_index("seq")
    tp = lax.axis_index("tp")
    chip = me // 2
    core = me % 2
    yy = chip // ZS
    zz = chip % ZS
    sibling = (me + 1 - 2 * core, tp)

    def chip_at(dy, dz):
        return (yy + dy) % YS * ZS + (zz + dz) % ZS

    chips = [chip_at(dy, dz) for dy, dz in OFFSETS]
    crossed = [(2 * chip_at(dy, 0) + 1 - core, tp) for dy in (2, 1, 3)]
    tps = [(me, (tp + d) % 4) for d in (2, 1, 3)]

    barrier = pltpu.get_barrier_semaphore()
    peers = [(2 * c + core, tp) for c in chips] + crossed + tps + [sibling]
    for p in peers:
        pl.semaphore_signal(barrier, inc=1, device_id=p, device_id_type=MESH)

    loads = [
        pltpu.make_async_copy(src, dst, load_sem.at[i])
        for i, (src, dst) in enumerate(
            ((k_hbm, k), (v_hbm, v), (q_hbm, q), (g_hbm, g), (gain_hbm, gain))
        )
    ]
    for load in loads:
        load.start()

    def remote(src, dst, index, device):
        return pltpu.make_async_remote_copy(
            src_ref=src, dst_ref=dst, send_sem=send_sem.at[index], recv_sem=recv_sem.at[index],
            device_id=device, device_id_type=MESH,
        )

    def rows(i, n):
        return pl.ds(pl.multiple_of(i * n, n), n)

    row_id = lax.broadcasted_iota(jnp.int32, (HALF, HALF), 0)
    col_id = lax.broadcasted_iota(jnp.int32, (HALF, HALF), 1)
    causal = col_id <= row_id
    eye = (
        lax.broadcasted_iota(jnp.int32, (HEAD_DIM, HEAD_DIM), 0)
        == lax.broadcasted_iota(jnp.int32, (HEAD_DIM, HEAD_DIM), 1)
    )
    mine = rows(core, HALF)
    other = rows(1 - core, HALF)
    own_heads = [2 * core, 2 * core + 1]
    other_heads = [2 - 2 * core, 3 - 2 * core]

    def where_at(u):
        b = u // NH
        h = u % NH
        start = pl.multiple_of(b * BLK, BLK)
        return b, h, start, rows(h, HEAD_DIM)

    def states(heads, left, right, scan, inner):
        for h in heads:
            cols = rows(h, HEAD_DIM)
            first = dot_tn(left[pl.ds(0, BLK), cols], right[pl.ds(0, BLK), cols])
            second = dot_tn(left[pl.ds(BLK, BLK), cols], right[pl.ds(BLK, BLK), cols])
            inside[scan, cols, :] = second if inner == 1 else first
            total[scan, cols, :] = first + second

    def score_unit(u, carry):
        b, h, start, cols = where_at(u)
        upper, lower, both = pl.ds(start, HALF), pl.ds(start + HALF, HALF), pl.ds(start, BLK)
        top = jnp.where(causal, dot_nt(q[upper, cols], k[upper, cols]), 0.0).astype(BF16)
        low = dot_nt(q[lower, cols], k[upper, cols]).astype(BF16)
        end = jnp.where(causal, dot_nt(q[lower, cols], k[lower, cols]), 0.0).astype(BF16)
        sc[u, pl.ds(0, HALF), pl.ds(0, HALF)] = top
        sc[u, pl.ds(HALF, HALF), pl.ds(0, HALF)] = low
        sc[u, pl.ds(HALF, HALF), pl.ds(HALF, HALF)] = end
        att[upper, cols] = dot_nn(top, v[upper, cols])
        att[lower, cols] = dot_nn(low, v[upper, cols]) + dot_nn(end, v[lower, cols])
        scaled[both, cols] = gain[:, cols] * g[both, cols].astype(F32)
        return carry

    def mixing_unit(u, carry):
        b, h, start, cols = where_at(u)
        upper, lower, both = pl.ds(start, HALF), pl.ds(start + HALF, HALF), pl.ds(start, BLK)
        d_up, d_low = da[upper, cols], da[lower, cols]
        top = jnp.where(causal, dot_nt(d_up, v[upper, cols]), 0.0).astype(BF16)
        low = dot_nt(d_low, v[upper, cols]).astype(BF16)
        end = jnp.where(causal, dot_nt(d_low, v[lower, cols]), 0.0).astype(BF16)
        before = pref[0, b, cols, :]
        k_up, k_low = k[upper, cols], k[lower, cols]
        qg_ref[upper, cols] = (dot_nt(d_up, before) + dot_nn(top, k_up)).astype(BF16)
        qg_ref[lower, cols] = (
            dot_nt(d_low, before) + dot_nn(low, k_up) + dot_nn(end, k_low)
        ).astype(BF16)
        q_up, q_low = q[upper, cols], q[lower, cols]
        kga[upper, cols] = dot_tn(top, q_up) + dot_tn(low, q_low)
        kga[lower, cols] = dot_tn(end, q_low)
        s_top = sc[u, pl.ds(0, HALF), pl.ds(0, HALF)]
        s_low = sc[u, pl.ds(HALF, HALF), pl.ds(0, HALF)]
        s_end = sc[u, pl.ds(HALF, HALF), pl.ds(HALF, HALF)]
        vga[upper, cols] = dot_tn(s_top, d_up) + dot_tn(s_low, d_low)
        vga[lower, cols] = dot_tn(s_end, d_low)
        return carry

    nothing = (CHIPS - 1) * PIECE

    def give_half(scan, base):
        give = remote(total.at[scan, other], sib.at[scan], base, sibling)
        give.start()
        return give

    def spread(scan, base, give):
        give.wait_recv()
        piece[scan] = total[scan, mine, :] + sib[scan]
        for c in chips:
            remote(
                piece.at[scan, rows(c, PIECE)], rb1.at[scan, rows(chip, PIECE)], base + 1, (2 * c + core, tp)
            ).start()
        rb1[scan, rows(chip, PIECE), :] = piece[scan, rows(chip, PIECE), :]
        return remote(piece.at[scan, pl.ds(0, nothing)], rb1.at[scan, pl.ds(0, nothing)], base + 1, sibling)

    def scan_back(scan, base, forward, wait1):
        wait1.wait_recv()
        running = jnp.zeros((PIECE, HEAD_DIM), F32)
        for i in range(CHIPS):
            at = pl.ds((i if forward else CHIPS - 1 - i) * PIECE, PIECE)
            ob1[scan, at, :] = running
            running = running + rb1[scan, at, :]
        for c in chips:
            remote(
                ob1.at[scan, rows(c, PIECE)], rb2.at[scan, rows(chip, PIECE)], base + 2, (2 * c + core, tp)
            ).start()
        rb2[scan, rows(chip, PIECE), :] = ob1[scan, rows(chip, PIECE), :]
        return remote(ob1.at[scan, pl.ds(0, nothing)], rb2.at[scan, pl.ds(0, nothing)], base + 2, sibling)

    def round_half(scan, half, forward):
        reach = edge[scan, half, :]
        further = (reach + inside[scan, half, :]).astype(BF16)
        pref[scan, 0 if forward else 1, half, :] = reach.astype(BF16)
        pref[scan, 1 if forward else 0, half, :] = further

    def swap_half(scan, base, forward, wait2):
        wait2.wait_recv()
        late = core == 1 if forward else core == 0
        arrived = rb2[scan]
        xb[scan] = arrived + jnp.where(late, 0.0, total[scan, mine, :])
        swap = remote(xb.at[scan], edge.at[scan, mine], base + 3, sibling)
        swap.start()
        edge[scan, mine, :] = arrived + jnp.where(late, sib[scan], 0.0)
        round_half(scan, mine, forward)
        return swap

    loads[0].wait()
    loads[1].wait()
    states(other_heads + own_heads, k, v, 0, 0)
    pl.semaphore_wait(barrier, len(peers))
    give = give_half(0, 0)
    loads[2].wait()
    loads[3].wait()
    loads[4].wait()
    wait1 = spread(0, 0, give)
    lax.fori_loop(0, FIRST_SPLIT, score_unit, 0)
    wait2 = scan_back(0, 0, True, wait1)
    lax.fori_loop(FIRST_SPLIT, 2 * NH, score_unit, 0)
    swap = swap_half(0, 0, True, wait2)

    def attend(heads, second):
        def body(i, carry):
            b = i // (BLK // HEAD_DIM)
            here = rows(i, HEAD_DIM)
            squares, inner = (rcol[here], mcol[here]) if second else (0.0, 0.0)
            for h in heads:
                cols = rows(h, HEAD_DIM)
                a = att[here, cols] + dot_nn(q[here, cols], pref[0, b, cols, :])
                att[here, cols] = a
                squares = squares + a * a
                inner = inner + scaled[here, cols] * a
            if second:
                sq = jnp.sum(squares, axis=1, keepdims=True)
                inn = jnp.sum(inner, axis=1, keepdims=True)
                tpo[pl.ds(i, 1), :] = jnp.sum(jnp.where(eye, sq, 0.0), axis=0, keepdims=True)
                tpo[pl.ds(i + 8, 1), :] = jnp.sum(jnp.where(eye, inn, 0.0), axis=0, keepdims=True)
            else:
                rcol[here] = squares
                mcol[here] = inner
            return carry

        lax.fori_loop(0, TOK // HEAD_DIM, body, 0, unroll=UNROLL)

    attend(own_heads, False)
    swap.wait_recv()
    round_half(0, other, True)
    attend(other_heads, True)
    sends = [remote(tpo, tpr.at[i], 11 + i, t) for i, t in enumerate(tps)]
    for s in sends:
        s.start()
    give.wait_send()
    wait1.wait_send()
    wait2.wait_send()
    swap.wait_send()
    for s in sends:
        s.wait_recv()
    sums = tpo[...] + tpr[0] + tpr[1] + tpr[2]
    for s in sends:
        s.wait_send()
    inverse = lax.rsqrt(sums[:8] / FULL + EPS)
    tpo[pl.ds(0, 8), :] = inverse
    tpo[pl.ds(8, 8), :] = inverse * inverse * inverse * (sums[8:] / FULL)

    def grads(heads, second):
        def body(i, carry):
            here = rows(i, HEAD_DIM)
            if second:
                r, m = rcol[here], mcol[here]
            else:
                r = jnp.sum(jnp.where(eye, tpo[pl.ds(i, 1), :], 0.0), axis=1, keepdims=True)
                m = jnp.sum(jnp.where(eye, tpo[pl.ds(i + 8, 1), :], 0.0), axis=1, keepdims=True)
                r = jnp.broadcast_to(r, (HEAD_DIM, HEAD_DIM))
                m = jnp.broadcast_to(m, (HEAD_DIM, HEAD_DIM))
                rcol[here] = r
                mcol[here] = m
            for h in heads:
                cols = rows(h, HEAD_DIM)
                da[here, cols] = (r * scaled[here, cols] - m * att[here, cols]).astype(BF16)
            return carry

        lax.fori_loop(0, TOK // HEAD_DIM, body, 0, unroll=UNROLL)

    grads(other_heads, False)
    states(other_heads, q, da, 1, 1)
    give = give_half(1, 4)
    grads(own_heads, True)
    states(own_heads, q, da, 1, 1)
    wait1 = spread(1, 4, give)

    def gains(i, carry):
        here = rows(i, HEAD_DIM)
        r = rcol[here]
        sums = []
        for h in range(NH):
            cols = pl.ds(h * HEAD_DIM, HEAD_DIM)
            term = g[here, cols].astype(F32) * att[here, cols] * r
            sums.append(carry[h] + jnp.sum(term.reshape(HEAD_DIM // 8, 8, HEAD_DIM), axis=0))
        return tuple(sums)

    zero = jnp.zeros((8, HEAD_DIM), F32)
    parts = lax.fori_loop(0, TOK // HEAD_DIM, gains, (zero,) * NH)
    for h in range(NH):
        gchip[pl.ds(h, 1), :] = jnp.sum(parts[h], axis=0, keepdims=True)
        gchip[pl.ds(h + NH, 1), :] = jnp.zeros((1, HEAD_DIM), F32)
    for d in (4, 3, 5, 2, 6, 1, 7):
        c = chip_at(0, d)
        remote(gchip, gz.at[zz], 8, (2 * c + core, tp)).start()
    gz[zz] = gchip[...]
    lax.fori_loop(0, SECOND_SPLIT, mixing_unit, 0)
    wait2 = scan_back(1, 4, False, wait1)
    wait_z = remote(gz.at[pl.ds(0, ZS - 1)], gz.at[pl.ds(0, ZS - 1)], 8, sibling)
    wait_z.wait_recv()
    gzs[...] = jnp.sum(gz[...], axis=0)
    for p in crossed + [(2 * chip_at(d, 0) + core, tp) for d in (2, 1, 3)] + [sibling]:
        remote(gzs, gy.at[2 * yy + core], 9, p).start()
    gy[2 * yy + core] = gzs[...]
    lax.fori_loop(SECOND_SPLIT, 2 * NH, mixing_unit, 0)
    swap = swap_half(1, 4, False, wait2)

    def finish(heads):
        for h in heads:
            cols = rows(h, HEAD_DIM)
            for b in range(2):
                both = pl.ds(b * BLK, BLK)
                after = pref[1, b, cols, :]
                kg_ref[both, cols] = (dot_nt(v[both, cols], after) + kga[both, cols]).astype(BF16)
                vg_ref[both, cols] = (dot_nn(k[both, cols], after) + vga[both, cols]).astype(BF16)

    finish(own_heads)
    wait_y = remote(gy.at[pl.ds(0, 2 * YS - 1)], gy.at[pl.ds(0, 2 * YS - 1)], 9, sibling)
    wait_y.wait_recv()
    gg_ref[...] = jnp.sum(gy[...], axis=0)[:NH]
    give.wait_send()
    wait1.wait_send()
    wait2.wait_send()
    wait_z.wait_send()
    wait_y.wait_send()
    swap.wait_recv()
    round_half(1, other, False)
    finish(other_heads)
    swap.wait_send()


def deliver(qg, kg, vg, gg, qg_hbm, kg_hbm, vg_hbm, gg_hbm, sem):
    copies = [
        pltpu.make_async_copy(src, dst, sem.at[i])
        for i, (src, dst) in enumerate(((qg, qg_hbm), (kg, kg_hbm), (vg, vg_hbm), (gg, gg_hbm)))
    ]
    for copy in copies:
        copy.start()
    for copy in copies:
        copy.wait()


def local(queries, keys, values, out_grad, gain):
    vmem = pltpu.VMEM
    big = jax.ShapeDtypeStruct((TOK, FEAT), BF16)
    state = (2, NH * HEAD_DIM, HEAD_DIM)
    half = (2, HALF, HEAD_DIM)
    tile = (8, HEAD_DIM)
    outside = pl.BlockSpec(memory_space=pltpu.HBM)
    whole = pl.BlockSpec(memory_space=vmem)
    results = (big, big, big, jax.ShapeDtypeStruct((NH, HEAD_DIM), F32))
    out = pl.pallas_call(
        kernel,
        name="attention_backward",
        out_shape=results,
        in_specs=[outside] * 5,
        out_specs=(whole,) * 4,
        scratch_shapes=[
            vmem((TOK, FEAT), BF16),
            vmem((TOK, FEAT), BF16),
            vmem((TOK, FEAT), BF16),
            vmem((TOK, FEAT), BF16),
            vmem((1, FEAT), F32),
            vmem((2 * NH, BLK, BLK), BF16),
            vmem((TOK, FEAT), F32),
            vmem((TOK, FEAT), F32),
            vmem((TOK, FEAT), BF16),
            vmem((TOK, FEAT), F32),
            vmem((TOK, FEAT), F32),
            vmem((TOK, HEAD_DIM), F32),
            vmem((TOK, HEAD_DIM), F32),
            vmem(state, F32),
            vmem(state, F32),
            vmem(half, F32),
            vmem(half, F32),
            vmem(half, F32),
            vmem(half, F32),
            vmem(half, F32),
            vmem(half, F32),
            vmem(state, F32),
            vmem((2,) + state, BF16),
            vmem((16, HEAD_DIM), F32),
            vmem((3, 16, HEAD_DIM), F32),
            vmem(tile, F32),
            vmem((ZS, 8, HEAD_DIM), F32),
            vmem(tile, F32),
            vmem((2 * YS, 8, HEAD_DIM), F32),
            pltpu.SemaphoreType.DMA((5,)),
            pltpu.SemaphoreType.DMA((14,)),
            pltpu.SemaphoreType.DMA((14,)),
        ],
        compiler_params=pltpu.CompilerParams(
            collective_id=0, has_side_effects=True, vmem_limit_bytes=53000000
        ),
    )(queries, keys, values, out_grad, gain.reshape(1, FEAT))
    out = pl.pallas_call(
        deliver,
        name="deliver",
        out_shape=results,
        in_specs=[whole] * 4,
        out_specs=(outside,) * 4,
        scratch_shapes=[pltpu.SemaphoreType.DMA((4,))],
        compiler_params=pltpu.CompilerParams(vmem_limit_bytes=1024 * 1024),
    )(*out)
    return out[0], out[1], out[2], out[3].reshape(FEAT)


def solution(mesh):
    in_specs = (P("seq", "tp"), P("seq", "tp"), P("seq", "tp"), P("seq", "tp"), P("tp"))
    out_specs = (P("seq", "tp"), P("seq", "tp"), P("seq", "tp"), P("tp"))
    return jax.shard_map(local, mesh=mesh, in_specs=in_specs, out_specs=out_specs, check_vma=False)
```

```python
import jax
import jax.numpy as jnp
from jax import lax
from jax.experimental import pallas as pl
from jax.experimental.pallas import tpu as pltpu
from jax.sharding import PartitionSpec as P

HEAD_DIM = 128
BLK = 512
HALF = 256
NH = 4
TOK = 1024
FEAT = 512
FULL = 2048.0
YS = 4
ZS = 8
CHIPS = YS * ZS
PIECE = 8
EPS = 1e-05
MESH = pl.DeviceIdType.MESH
F32 = jnp.float32
BF16 = jnp.bfloat16

FIRST_SPLIT = 5
SECOND_SPLIT = 4


def ring(n, d):
    return min(d, n - d)


OFFSETS = sorted(
    [(dy, dz) for dy in range(YS) for dz in range(ZS) if (dy, dz) != (0, 0)],
    key=lambda o: -(ring(YS, o[0]) + ring(ZS, o[1])),
)


def dot_nn(a, b):
    return lax.dot_general(a, b, (((1,), (0,)), ((), ())), preferred_element_type=F32)


def dot_nt(a, b):
    return lax.dot_general(a, b, (((1,), (1,)), ((), ())), preferred_element_type=F32)


def dot_tn(a, b):
    return lax.dot_general(a, b, (((0,), (0,)), ((), ())), preferred_element_type=F32)


def kernel(
    q_hbm, k_hbm, v_hbm, g_hbm, gain_hbm,
    qg_ref, kg_ref, vg_ref, gg_ref, k, v, kga, vga, after_ref,
    q, g, gain, sc, att, scaled, da, rcol, mcol,
    inside, total, sib, piece, rb1, ob1, rb2, xb, edge, pref,
    tpo, tpr, coef, gchip, gz, gzs, gy,
    load_sem, send_sem, recv_sem,
):
    me = lax.axis_index("seq")
    tp = lax.axis_index("tp")
    chip = me // 2
    core = me % 2
    yy = chip // ZS
    zz = chip % ZS
    sibling = (me + 1 - 2 * core, tp)

    def chip_at(dy, dz):
        return (yy + dy) % YS * ZS + (zz + dz) % ZS

    chips = [chip_at(dy, dz) for dy, dz in OFFSETS]
    crossed = [(2 * chip_at(dy, 0) + 1 - core, tp) for dy in (2, 1, 3)]
    tps = [(me, (tp + d) % 4) for d in (2, 1, 3)]

    barrier = pltpu.get_barrier_semaphore()
    peers = [(2 * c + core, tp) for c in chips] + crossed + tps + [sibling]
    for p in peers:
        pl.semaphore_signal(barrier, inc=1, device_id=p, device_id_type=MESH)

    loads = [
        pltpu.make_async_copy(src, dst, load_sem.at[i])
        for i, (src, dst) in enumerate(
            ((k_hbm, k), (v_hbm, v), (q_hbm, q), (g_hbm, g), (gain_hbm, gain))
        )
    ]
    loads[0].start()
    loads[1].start()

    def remote(src, dst, index, device):
        return pltpu.make_async_remote_copy(
            src_ref=src, dst_ref=dst, send_sem=send_sem.at[index], recv_sem=recv_sem.at[index],
            device_id=device, device_id_type=MESH,
        )

    def rows(i, n):
        return pl.ds(pl.multiple_of(i * n, n), n)

    row_id = lax.broadcasted_iota(jnp.int32, (HALF, HALF), 0)
    col_id = lax.broadcasted_iota(jnp.int32, (HALF, HALF), 1)
    causal = col_id <= row_id
    eye = (
        lax.broadcasted_iota(jnp.int32, (HEAD_DIM, HEAD_DIM), 0)
        == lax.broadcasted_iota(jnp.int32, (HEAD_DIM, HEAD_DIM), 1)
    )
    mine = rows(core, HALF)
    other = rows(1 - core, HALF)
    own_heads = [2 * core, 2 * core + 1]
    other_heads = [2 - 2 * core, 3 - 2 * core]

    def where_at(u):
        b = u // NH
        h = u % NH
        start = pl.multiple_of(b * BLK, BLK)
        return b, h, start, rows(h, HEAD_DIM)

    def states(heads, left, right, scan, inner):
        for h in heads:
            cols = rows(h, HEAD_DIM)
            first = dot_tn(left[pl.ds(0, BLK), cols], right[pl.ds(0, BLK), cols])
            second = dot_tn(left[pl.ds(BLK, BLK), cols], right[pl.ds(BLK, BLK), cols])
            inside[scan, cols, :] = second if inner == 1 else first
            total[scan, cols, :] = first + second

    def score_unit(u, carry):
        b, h, start, cols = where_at(u)
        upper, lower, both = pl.ds(start, HALF), pl.ds(start + HALF, HALF), pl.ds(start, BLK)
        top = jnp.where(causal, dot_nt(q[upper, cols], k[upper, cols]), 0.0).astype(BF16)
        low = dot_nt(q[lower, cols], k[upper, cols]).astype(BF16)
        end = jnp.where(causal, dot_nt(q[lower, cols], k[lower, cols]), 0.0).astype(BF16)
        sc[u, pl.ds(0, HALF), pl.ds(0, HALF)] = top
        sc[u, pl.ds(HALF, HALF), pl.ds(0, HALF)] = low
        sc[u, pl.ds(HALF, HALF), pl.ds(HALF, HALF)] = end
        att[upper, cols] = dot_nn(top, v[upper, cols])
        att[lower, cols] = dot_nn(low, v[upper, cols]) + dot_nn(end, v[lower, cols])
        scaled[both, cols] = gain[:, cols] * g[both, cols].astype(F32)
        return carry

    def mixing_unit(u, carry):
        b, h, start, cols = where_at(u)
        upper, lower, both = pl.ds(start, HALF), pl.ds(start + HALF, HALF), pl.ds(start, BLK)
        d_up, d_low = da[upper, cols], da[lower, cols]
        top = jnp.where(causal, dot_nt(d_up, v[upper, cols]), 0.0).astype(BF16)
        low = dot_nt(d_low, v[upper, cols]).astype(BF16)
        end = jnp.where(causal, dot_nt(d_low, v[lower, cols]), 0.0).astype(BF16)
        before = pref[b, cols, :]
        k_up, k_low = k[upper, cols], k[lower, cols]
        qg_ref[upper, cols] = (dot_nt(d_up, before) + dot_nn(top, k_up)).astype(BF16)
        qg_ref[lower, cols] = (
            dot_nt(d_low, before) + dot_nn(low, k_up) + dot_nn(end, k_low)
        ).astype(BF16)
        q_up, q_low = q[upper, cols], q[lower, cols]
        kga[upper, cols] = dot_tn(top, q_up) + dot_tn(low, q_low)
        kga[lower, cols] = dot_tn(end, q_low)
        s_top = sc[u, pl.ds(0, HALF), pl.ds(0, HALF)]
        s_low = sc[u, pl.ds(HALF, HALF), pl.ds(0, HALF)]
        s_end = sc[u, pl.ds(HALF, HALF), pl.ds(HALF, HALF)]
        vga[upper, cols] = dot_tn(s_top, d_up) + dot_tn(s_low, d_low)
        vga[lower, cols] = dot_tn(s_end, d_low)
        return carry

    nothing = (CHIPS - 1) * PIECE

    def give_half(scan, base):
        give = remote(total.at[scan, other], sib.at[scan], base, sibling)
        give.start()
        return give

    def spread(scan, base, give):
        give.wait_recv()
        piece[scan] = total[scan, mine, :] + sib[scan]
        for c in chips:
            remote(
                piece.at[scan, rows(c, PIECE)], rb1.at[scan, rows(chip, PIECE)], base + 1, (2 * c + core, tp)
            ).start()
        rb1[scan, rows(chip, PIECE), :] = piece[scan, rows(chip, PIECE), :]
        return remote(piece.at[scan, pl.ds(0, nothing)], rb1.at[scan, pl.ds(0, nothing)], base + 1, sibling)

    def scan_back(scan, base, forward, wait1):
        wait1.wait_recv()
        running = jnp.zeros((PIECE, HEAD_DIM), F32)
        for i in range(CHIPS):
            at = pl.ds((i if forward else CHIPS - 1 - i) * PIECE, PIECE)
            ob1[scan, at, :] = running
            running = running + rb1[scan, at, :]
        for c in chips:
            remote(
                ob1.at[scan, rows(c, PIECE)], rb2.at[scan, rows(chip, PIECE)], base + 2, (2 * c + core, tp)
            ).start()
        rb2[scan, rows(chip, PIECE), :] = ob1[scan, rows(chip, PIECE), :]
        return remote(ob1.at[scan, pl.ds(0, nothing)], rb2.at[scan, pl.ds(0, nothing)], base + 2, sibling)

    def round_half(scan, half, forward):
        reach = edge[scan, half, :]
        further = (reach + inside[scan, half, :]).astype(BF16)
        into = pref if forward else after_ref
        into[0 if forward else 1, half, :] = reach.astype(BF16)
        into[1 if forward else 0, half, :] = further

    def swap_half(scan, base, forward, wait2):
        wait2.wait_recv()
        late = core == 1 if forward else core == 0
        arrived = rb2[scan]
        xb[scan] = arrived + jnp.where(late, 0.0, total[scan, mine, :])
        swap = remote(xb.at[scan], edge.at[scan, mine], base + 3, sibling)
        swap.start()
        edge[scan, mine, :] = arrived + jnp.where(late, sib[scan], 0.0)
        round_half(scan, mine, forward)
        return swap

    loads[0].wait()
    loads[1].wait()
    for load in loads[2:]:
        load.start()
    states(other_heads + own_heads, k, v, 0, 0)
    pl.semaphore_wait(barrier, len(peers))
    give = give_half(0, 0)
    loads[2].wait()
    loads[3].wait()
    loads[4].wait()
    wait1 = spread(0, 0, give)
    lax.fori_loop(0, FIRST_SPLIT, score_unit, 0)
    wait2 = scan_back(0, 0, True, wait1)
    lax.fori_loop(FIRST_SPLIT, 2 * NH, score_unit, 0)
    swap = swap_half(0, 0, True, wait2)

    groups = BLK // HEAD_DIM

    def attend(heads, second, b):
        def body(j, carry):
            here = rows(b * groups + j, HEAD_DIM)
            squares, inner = (rcol[here], mcol[here]) if second else (0.0, 0.0)
            for h in heads:
                cols = rows(h, HEAD_DIM)
                a = att[here, cols] + dot_nn(q[here, cols], pref[b, cols, :])
                att[here, cols] = a
                squares = squares + a * a
                inner = inner + scaled[here, cols] * a
            if second:
                sq = jnp.sum(squares, axis=1, keepdims=True)
                inn = jnp.sum(inner, axis=1, keepdims=True)
                tpo[b, pl.ds(j, 1), :] = jnp.sum(jnp.where(eye, sq, 0.0), axis=0, keepdims=True)
                tpo[b, pl.ds(j + groups, 1), :] = jnp.sum(
                    jnp.where(eye, inn, 0.0), axis=0, keepdims=True
                )
            else:
                rcol[here] = squares
                mcol[here] = inner
            return carry

        lax.fori_loop(0, groups, body, 0, unroll=True)

    attend(own_heads, False, 0)
    attend(own_heads, False, 1)
    swap.wait_recv()
    round_half(0, other, True)
    sends = []
    for b in range(2):
        attend(other_heads, True, b)
        sends.append([remote(tpo.at[b], tpr.at[i, b], 11 + 3 * b + i, t) for i, t in enumerate(tps)])
        for x in sends[b]:
            x.start()
    give.wait_send()
    wait1.wait_send()
    wait2.wait_send()
    swap.wait_send()

    def grads(heads, second, b):
        def body(j, carry):
            here = rows(b * groups + j, HEAD_DIM)
            if second:
                r, m = rcol[here], mcol[here]
            else:
                r = jnp.sum(jnp.where(eye, coef[b, pl.ds(j, 1), :], 0.0), axis=1, keepdims=True)
                m = jnp.sum(
                    jnp.where(eye, coef[b, pl.ds(j + groups, 1), :], 0.0), axis=1, keepdims=True
                )
                r = jnp.broadcast_to(r, (HEAD_DIM, HEAD_DIM))
                m = jnp.broadcast_to(m, (HEAD_DIM, HEAD_DIM))
                rcol[here] = r
                mcol[here] = m
            for h in heads:
                cols = rows(h, HEAD_DIM)
                da[here, cols] = (r * scaled[here, cols] - m * att[here, cols]).astype(BF16)
            return carry

        lax.fori_loop(0, groups, body, 0, unroll=True)

    for b in range(2):
        for x in sends[b]:
            x.wait_recv()
        sums = tpo[b] + tpr[0, b] + tpr[1, b] + tpr[2, b]
        inverse = lax.rsqrt(sums[:groups] / FULL + EPS)
        coef[b, pl.ds(0, groups), :] = inverse
        coef[b, pl.ds(groups, groups), :] = inverse * inverse * inverse * (sums[groups:] / FULL)
        grads(other_heads, False, b)
    states(other_heads, q, da, 1, 1)
    give = give_half(1, 4)
    grads(own_heads, True, 0)
    grads(own_heads, True, 1)
    states(own_heads, q, da, 1, 1)
    wait1 = spread(1, 4, give)

    def gains(i, carry):
        here = rows(i, HEAD_DIM)
        r = rcol[here]
        sums = []
        for h in range(NH):
            cols = pl.ds(h * HEAD_DIM, HEAD_DIM)
            term = g[here, cols].astype(F32) * att[here, cols] * r
            sums.append(carry[h] + jnp.sum(term.reshape(HEAD_DIM // 8, 8, HEAD_DIM), axis=0))
        return tuple(sums)

    zero = jnp.zeros((8, HEAD_DIM), F32)
    parts = lax.fori_loop(0, TOK // HEAD_DIM, gains, (zero,) * NH)
    for h in range(NH):
        gchip[pl.ds(h, 1), :] = jnp.sum(parts[h], axis=0, keepdims=True)
        gchip[pl.ds(h + NH, 1), :] = jnp.zeros((1, HEAD_DIM), F32)
    for d in (4, 3, 5, 2, 6, 1, 7):
        c = chip_at(0, d)
        remote(gchip, gz.at[zz], 8, (2 * c + core, tp)).start()
    gz[zz] = gchip[...]
    lax.fori_loop(0, SECOND_SPLIT, mixing_unit, 0)
    wait2 = scan_back(1, 4, False, wait1)
    wait_z = remote(gz.at[pl.ds(0, ZS - 1)], gz.at[pl.ds(0, ZS - 1)], 8, sibling)
    wait_z.wait_recv()
    gzs[...] = jnp.sum(gz[...], axis=0)
    for p in crossed + [(2 * chip_at(d, 0) + core, tp) for d in (2, 1, 3)] + [sibling]:
        remote(gzs, gy.at[2 * yy + core], 9, p).start()
    gy[2 * yy + core] = gzs[...]
    lax.fori_loop(SECOND_SPLIT, 2 * NH, mixing_unit, 0)
    swap = swap_half(1, 4, False, wait2)

    for n, h in enumerate(own_heads):
        cols, to = rows(h, HEAD_DIM), pl.ds(n * HEAD_DIM, HEAD_DIM)
        for b in range(2):
            both = pl.ds(b * BLK, BLK)
            after = after_ref[b, cols, :]
            kg_ref[both, to] = (dot_nt(v[both, cols], after) + kga[both, cols]).astype(BF16)
            vg_ref[both, to] = (dot_nn(k[both, cols], after) + vga[both, cols]).astype(BF16)
    wait_y = remote(gy.at[pl.ds(0, 2 * YS - 1)], gy.at[pl.ds(0, 2 * YS - 1)], 9, sibling)
    wait_y.wait_recv()
    gg_ref[...] = jnp.sum(gy[...], axis=0)[:NH]
    give.wait_send()
    wait1.wait_send()
    wait2.wait_send()
    wait_z.wait_send()
    wait_y.wait_send()
    for x in sends[0] + sends[1]:
        x.wait_send()
    swap.wait_recv()
    round_half(1, other, False)
    swap.wait_send()


def deliver(
    qg, kg, vg, gg, k, v, kga, vga, after_ref,
    qg_hbm, kg_hbm, vg_hbm, gg_hbm,
    kgo, vgo, sem,
):
    core = lax.axis_index("seq") % 2
    own = pl.ds(pl.multiple_of(core * HALF, HALF), HALF)
    other = pl.ds(pl.multiple_of((1 - core) * HALF, HALF), HALF)
    copies = []

    def send(src, dst):
        copies.append(pltpu.make_async_copy(src, dst, sem.at[len(copies)]))
        copies[-1].start()

    send(qg, qg_hbm)
    send(kg, kg_hbm.at[:, own])
    send(vg, vg_hbm.at[:, own])
    send(gg, gg_hbm)
    for b in range(2):
        both = pl.ds(b * BLK, BLK)
        for n in range(2):
            cols = pl.ds(pl.multiple_of((2 - 2 * core + n) * HEAD_DIM, HEAD_DIM), HEAD_DIM)
            to = pl.ds(n * HEAD_DIM, HEAD_DIM)
            after = after_ref[b, cols, :]
            kgo[both, to] = (dot_nt(v[both, cols], after) + kga[both, cols]).astype(BF16)
            vgo[both, to] = (dot_nn(k[both, cols], after) + vga[both, cols]).astype(BF16)
        send(kgo.at[both], kg_hbm.at[both, other])
        send(vgo.at[both], vg_hbm.at[both, other])
    for copy in copies:
        copy.wait()


def local(queries, keys, values, out_grad, gain):
    vmem = pltpu.VMEM
    big = jax.ShapeDtypeStruct((TOK, FEAT), BF16)
    state = (2, NH * HEAD_DIM, HEAD_DIM)
    half = (2, HALF, HEAD_DIM)
    tile = (8, HEAD_DIM)
    outside = pl.BlockSpec(memory_space=pltpu.HBM)
    whole = pl.BlockSpec(memory_space=vmem)
    results = (big, big, big, jax.ShapeDtypeStruct((NH, HEAD_DIM), F32))
    part = vmem((TOK, HALF), BF16)
    entire = vmem((TOK, FEAT), BF16)
    wide = vmem((TOK, FEAT), F32)
    kept = (
        entire, part, part, vmem((NH, HEAD_DIM), F32), entire, entire, wide, wide, vmem(state, BF16)
    )
    out = pl.pallas_call(
        kernel,
        name="attention_backward",
        out_shape=kept,
        in_specs=[outside] * 5,
        out_specs=(whole,) * len(kept),
        scratch_shapes=[
            vmem((TOK, FEAT), BF16),
            vmem((TOK, FEAT), BF16),
            vmem((1, FEAT), F32),
            vmem((2 * NH, BLK, BLK), BF16),
            vmem((TOK, FEAT), F32),
            vmem((TOK, FEAT), F32),
            vmem((TOK, FEAT), BF16),
            vmem((TOK, HEAD_DIM), F32),
            vmem((TOK, HEAD_DIM), F32),
            vmem(state, F32),
            vmem(state, F32),
            vmem(half, F32),
            vmem(half, F32),
            vmem(half, F32),
            vmem(half, F32),
            vmem(half, F32),
            vmem(half, F32),
            vmem(state, F32),
            vmem(state, BF16),
            vmem((2,) + tile, F32),
            vmem((3, 2) + tile, F32),
            vmem((2,) + tile, F32),
            vmem(tile, F32),
            vmem((ZS, 8, HEAD_DIM), F32),
            vmem(tile, F32),
            vmem((2 * YS, 8, HEAD_DIM), F32),
            pltpu.SemaphoreType.DMA((5,)),
            pltpu.SemaphoreType.DMA((17,)),
            pltpu.SemaphoreType.DMA((17,)),
        ],
        compiler_params=pltpu.CompilerParams(
            collective_id=0, has_side_effects=True, vmem_limit_bytes=40 * 1024 * 1024
        ),
    )(*(
        pltpu.with_memory_space_constraint(x, pltpu.HBM)
        for x in (queries, keys, values, out_grad, gain.reshape(1, FEAT))
    ))
    out = pl.pallas_call(
        deliver,
        name="deliver",
        out_shape=results,
        in_specs=[whole] * len(kept),
        out_specs=(outside,) * 4,
        scratch_shapes=[part, part, pltpu.SemaphoreType.DMA((8,))],
        compiler_params=pltpu.CompilerParams(vmem_limit_bytes=20 * 1024 * 1024),
    )(*out)
    return out[0], out[1], out[2], out[3].reshape(FEAT)


def solution(mesh):
    in_specs = (P("seq", "tp"), P("seq", "tp"), P("seq", "tp"), P("seq", "tp"), P("tp"))
    out_specs = (P("seq", "tp"), P("seq", "tp"), P("seq", "tp"), P("tp"))
    return jax.shard_map(local, mesh=mesh, in_specs=in_specs, out_specs=out_specs, check_vma=False)
```

```python
import jax
import jax.numpy as jnp
from jax import lax
from jax.experimental import pallas as pl
from jax.experimental.pallas import tpu as pltpu
from jax.sharding import PartitionSpec as P

HEAD_DIM = 128
BLK = 512
HALF = 256
NH = 4
TOK = 1024
FEAT = 512
FULL = 2048.0
YS = 4
ZS = 8
CHIPS = YS * ZS
PIECE = 8
EPS = 1e-05
MESH = pl.DeviceIdType.MESH
F32 = jnp.float32
BF16 = jnp.bfloat16

FIRST_SPLIT = 5
SECOND_SPLIT = 4


def ring(n, d):
    return min(d, n - d)


OFFSETS = sorted(
    [(dy, dz) for dy in range(YS) for dz in range(ZS) if (dy, dz) != (0, 0)],
    key=lambda o: -(ring(YS, o[0]) + ring(ZS, o[1])),
)


def dot_nn(a, b):
    return lax.dot_general(a, b, (((1,), (0,)), ((), ())), preferred_element_type=F32)


def dot_nt(a, b):
    return lax.dot_general(a, b, (((1,), (1,)), ((), ())), preferred_element_type=F32)


def dot_tn(a, b):
    return lax.dot_general(a, b, (((0,), (0,)), ((), ())), preferred_element_type=F32)


def kernel(
    q_hbm, k_hbm, v_hbm, g_hbm, gain_hbm,
    qg_ref, kg_ref, vg_ref, gg_ref, k, v, kga, vga, after_ref,
    q, g, gain, sc, att, scaled, da, rcol, mcol,
    inside, total, sib, piece, rb1, ob1, rb2, xb, edge, pref,
    tpo, tpr, coef, gchip, gz, gzs, gy,
    load_sem, send_sem, recv_sem,
):
    me = lax.axis_index("seq")
    tp = lax.axis_index("tp")
    chip = me // 2
    core = me % 2
    yy = chip // ZS
    zz = chip % ZS
    sibling = (me + 1 - 2 * core, tp)

    def chip_at(dy, dz):
        return (yy + dy) % YS * ZS + (zz + dz) % ZS

    turn = 1 - 2 * core
    chips = [chip_at(YS + turn * dy, ZS + turn * dz) for dy, dz in OFFSETS]
    crossed = [(2 * chip_at(dy, 0) + 1 - core, tp) for dy in (2, 1, 3)]
    tps = [(me, (tp + d) % 4) for d in (2, 1, 3)]

    barrier = pltpu.get_barrier_semaphore()
    peers = [(2 * c + core, tp) for c in chips] + crossed + tps + [sibling]
    for p in peers:
        pl.semaphore_signal(barrier, inc=1, device_id=p, device_id_type=MESH)

    loads = [
        pltpu.make_async_copy(src, dst, load_sem.at[i])
        for i, (src, dst) in enumerate(
            ((k_hbm, k), (v_hbm, v), (q_hbm, q), (g_hbm, g), (gain_hbm, gain))
        )
    ]
    loads[0].start()
    loads[1].start()

    def remote(src, dst, index, device):
        return pltpu.make_async_remote_copy(
            src_ref=src, dst_ref=dst, send_sem=send_sem.at[index], recv_sem=recv_sem.at[index],
            device_id=device, device_id_type=MESH,
        )

    def rows(i, n):
        return pl.ds(pl.multiple_of(i * n, n), n)

    row_id = lax.broadcasted_iota(jnp.int32, (HALF, HALF), 0)
    col_id = lax.broadcasted_iota(jnp.int32, (HALF, HALF), 1)
    causal = col_id <= row_id
    eye = (
        lax.broadcasted_iota(jnp.int32, (HEAD_DIM, HEAD_DIM), 0)
        == lax.broadcasted_iota(jnp.int32, (HEAD_DIM, HEAD_DIM), 1)
    )
    mine = rows(core, HALF)
    other = rows(1 - core, HALF)
    own_heads = [2 * core, 2 * core + 1]
    other_heads = [2 - 2 * core, 3 - 2 * core]

    def where_at(u):
        b = u // NH
        h = u % NH
        start = pl.multiple_of(b * BLK, BLK)
        return b, h, start, rows(h, HEAD_DIM)

    def states(heads, left, right, scan, inner):
        for h in heads:
            cols = rows(h, HEAD_DIM)
            first = dot_tn(left[pl.ds(0, BLK), cols], right[pl.ds(0, BLK), cols])
            second = dot_tn(left[pl.ds(BLK, BLK), cols], right[pl.ds(BLK, BLK), cols])
            inside[scan, cols, :] = second if inner == 1 else first
            total[scan, cols, :] = first + second

    def score_unit(u, carry):
        b, h, start, cols = where_at(u)
        upper, lower, both = pl.ds(start, HALF), pl.ds(start + HALF, HALF), pl.ds(start, BLK)
        top = jnp.where(causal, dot_nt(q[upper, cols], k[upper, cols]), 0.0).astype(BF16)
        low = dot_nt(q[lower, cols], k[upper, cols]).astype(BF16)
        end = jnp.where(causal, dot_nt(q[lower, cols], k[lower, cols]), 0.0).astype(BF16)
        sc[u, pl.ds(0, HALF), pl.ds(0, HALF)] = top
        sc[u, pl.ds(HALF, HALF), pl.ds(0, HALF)] = low
        sc[u, pl.ds(HALF, HALF), pl.ds(HALF, HALF)] = end
        att[upper, cols] = dot_nn(top, v[upper, cols])
        att[lower, cols] = dot_nn(low, v[upper, cols]) + dot_nn(end, v[lower, cols])
        scaled[both, cols] = gain[:, cols] * g[both, cols].astype(F32)
        return carry

    def mixing_unit(u, carry):
        b, h, start, cols = where_at(u)
        upper, lower, both = pl.ds(start, HALF), pl.ds(start + HALF, HALF), pl.ds(start, BLK)
        d_up, d_low = da[upper, cols], da[lower, cols]
        top = jnp.where(causal, dot_nt(d_up, v[upper, cols]), 0.0).astype(BF16)
        low = dot_nt(d_low, v[upper, cols]).astype(BF16)
        end = jnp.where(causal, dot_nt(d_low, v[lower, cols]), 0.0).astype(BF16)
        before = pref[b, cols, :]
        k_up, k_low = k[upper, cols], k[lower, cols]
        qg_ref[upper, cols] = (dot_nt(d_up, before) + dot_nn(top, k_up)).astype(BF16)
        qg_ref[lower, cols] = (
            dot_nt(d_low, before) + dot_nn(low, k_up) + dot_nn(end, k_low)
        ).astype(BF16)
        q_up, q_low = q[upper, cols], q[lower, cols]
        kga[upper, cols] = dot_tn(top, q_up) + dot_tn(low, q_low)
        kga[lower, cols] = dot_tn(end, q_low)
        s_top = sc[u, pl.ds(0, HALF), pl.ds(0, HALF)]
        s_low = sc[u, pl.ds(HALF, HALF), pl.ds(0, HALF)]
        s_end = sc[u, pl.ds(HALF, HALF), pl.ds(HALF, HALF)]
        vga[upper, cols] = dot_tn(s_top, d_up) + dot_tn(s_low, d_low)
        vga[lower, cols] = dot_tn(s_end, d_low)
        return carry

    nothing = (CHIPS - 1) * PIECE

    def give_half(scan, base):
        give = remote(total.at[scan, other], sib.at[scan], base, sibling)
        give.start()
        return give

    def spread(scan, base, give):
        give.wait_recv()
        piece[scan] = total[scan, mine, :] + sib[scan]
        for c in chips:
            remote(
                piece.at[scan, rows(c, PIECE)], rb1.at[scan, rows(chip, PIECE)], base + 1, (2 * c + core, tp)
            ).start()
        rb1[scan, rows(chip, PIECE), :] = piece[scan, rows(chip, PIECE), :]
        return remote(piece.at[scan, pl.ds(0, nothing)], rb1.at[scan, pl.ds(0, nothing)], base + 1, sibling)

    def scan_back(scan, base, forward, wait1):
        wait1.wait_recv()
        running = jnp.zeros((PIECE, HEAD_DIM), F32)
        for i in range(CHIPS):
            at = pl.ds((i if forward else CHIPS - 1 - i) * PIECE, PIECE)
            ob1[scan, at, :] = running
            running = running + rb1[scan, at, :]
        for c in chips:
            remote(
                ob1.at[scan, rows(c, PIECE)], rb2.at[scan, rows(chip, PIECE)], base + 2, (2 * c + core, tp)
            ).start()
        rb2[scan, rows(chip, PIECE), :] = ob1[scan, rows(chip, PIECE), :]
        return remote(ob1.at[scan, pl.ds(0, nothing)], rb2.at[scan, pl.ds(0, nothing)], base + 2, sibling)

    def round_half(scan, half, forward):
        reach = edge[scan, half, :]
        further = (reach + inside[scan, half, :]).astype(BF16)
        into = pref if forward else after_ref
        into[0 if forward else 1, half, :] = reach.astype(BF16)
        into[1 if forward else 0, half, :] = further

    def swap_half(scan, base, forward, wait2):
        wait2.wait_recv()
        late = core == 1 if forward else core == 0
        arrived = rb2[scan]
        xb[scan] = arrived + jnp.where(late, 0.0, total[scan, mine, :])
        swap = remote(xb.at[scan], edge.at[scan, mine], base + 3, sibling)
        swap.start()
        edge[scan, mine, :] = arrived + jnp.where(late, sib[scan], 0.0)
        round_half(scan, mine, forward)
        return swap

    loads[0].wait()
    loads[1].wait()
    for load in loads[2:]:
        load.start()
    states(other_heads, k, v, 0, 0)
    pl.semaphore_wait(barrier, len(peers))
    give = give_half(0, 0)
    states(own_heads, k, v, 0, 0)
    loads[2].wait()
    loads[3].wait()
    loads[4].wait()
    wait1 = spread(0, 0, give)
    lax.fori_loop(0, FIRST_SPLIT, score_unit, 0)
    wait2 = scan_back(0, 0, True, wait1)
    lax.fori_loop(FIRST_SPLIT, 2 * NH, score_unit, 0)
    swap = swap_half(0, 0, True, wait2)

    groups = BLK // HEAD_DIM

    def attend(heads, second, b):
        def body(j, carry):
            here = rows(b * groups + j, HEAD_DIM)
            squares, inner = (rcol[here], mcol[here]) if second else (0.0, 0.0)
            for h in heads:
                cols = rows(h, HEAD_DIM)
                a = att[here, cols] + dot_nn(q[here, cols], pref[b, cols, :])
                att[here, cols] = a
                squares = squares + a * a
                inner = inner + scaled[here, cols] * a
            if second:
                sq = jnp.sum(squares, axis=1, keepdims=True)
                inn = jnp.sum(inner, axis=1, keepdims=True)
                tpo[b, pl.ds(j, 1), :] = jnp.sum(jnp.where(eye, sq, 0.0), axis=0, keepdims=True)
                tpo[b, pl.ds(j + groups, 1), :] = jnp.sum(
                    jnp.where(eye, inn, 0.0), axis=0, keepdims=True
                )
            else:
                rcol[here] = squares
                mcol[here] = inner
            return carry

        lax.fori_loop(0, groups, body, 0, unroll=True)

    attend(own_heads, False, 0)
    attend(own_heads, False, 1)
    swap.wait_recv()
    round_half(0, other, True)
    sends = []
    for b in range(2):
        attend(other_heads, True, b)
        sends.append([remote(tpo.at[b], tpr.at[i, b], 11 + 3 * b + i, t) for i, t in enumerate(tps)])
        for x in sends[b]:
            x.start()
    give.wait_send()
    wait1.wait_send()
    wait2.wait_send()
    swap.wait_send()

    def grads(heads, second, b):
        def body(j, carry):
            here = rows(b * groups + j, HEAD_DIM)
            if second:
                r, m = rcol[here], mcol[here]
            else:
                r = jnp.sum(jnp.where(eye, coef[b, pl.ds(j, 1), :], 0.0), axis=1, keepdims=True)
                m = jnp.sum(
                    jnp.where(eye, coef[b, pl.ds(j + groups, 1), :], 0.0), axis=1, keepdims=True
                )
                r = jnp.broadcast_to(r, (HEAD_DIM, HEAD_DIM))
                m = jnp.broadcast_to(m, (HEAD_DIM, HEAD_DIM))
                rcol[here] = r
                mcol[here] = m
            for h in heads:
                cols = rows(h, HEAD_DIM)
                da[here, cols] = (r * scaled[here, cols] - m * att[here, cols]).astype(BF16)
            return carry

        lax.fori_loop(0, groups, body, 0, unroll=True)

    for b in range(2):
        for x in sends[b]:
            x.wait_recv()
        sums = tpo[b] + tpr[0, b] + tpr[1, b] + tpr[2, b]
        inverse = lax.rsqrt(sums[:groups] / FULL + EPS)
        coef[b, pl.ds(0, groups), :] = inverse
        coef[b, pl.ds(groups, groups), :] = inverse * inverse * inverse * (sums[groups:] / FULL)
        grads(other_heads, False, b)
    states(other_heads, q, da, 1, 1)
    give = give_half(1, 4)
    grads(own_heads, True, 0)
    grads(own_heads, True, 1)
    states(own_heads, q, da, 1, 1)
    wait1 = spread(1, 4, give)

    def gains(i, carry):
        here = rows(i, HEAD_DIM)
        r = rcol[here]
        sums = []
        for h in range(NH):
            cols = pl.ds(h * HEAD_DIM, HEAD_DIM)
            term = g[here, cols].astype(F32) * att[here, cols] * r
            sums.append(carry[h] + jnp.sum(term.reshape(HEAD_DIM // 8, 8, HEAD_DIM), axis=0))
        return tuple(sums)

    zero = jnp.zeros((8, HEAD_DIM), F32)
    parts = lax.fori_loop(0, TOK // HEAD_DIM, gains, (zero,) * NH)
    for h in range(NH):
        gchip[pl.ds(h, 1), :] = jnp.sum(parts[h], axis=0, keepdims=True)
        gchip[pl.ds(h + NH, 1), :] = jnp.zeros((1, HEAD_DIM), F32)
    for d in (4, 3, 5, 2, 6, 1, 7):
        c = chip_at(0, d)
        remote(gchip, gz.at[zz], 8, (2 * c + core, tp)).start()
    gz[zz] = gchip[...]
    lax.fori_loop(0, SECOND_SPLIT, mixing_unit, 0)
    wait2 = scan_back(1, 4, False, wait1)
    wait_z = remote(gz.at[pl.ds(0, ZS - 1)], gz.at[pl.ds(0, ZS - 1)], 8, sibling)
    wait_z.wait_recv()
    gzs[...] = jnp.sum(gz[...], axis=0)
    for p in crossed + [(2 * chip_at(d, 0) + core, tp) for d in (2, 1, 3)] + [sibling]:
        remote(gzs, gy.at[2 * yy + core], 9, p).start()
    gy[2 * yy + core] = gzs[...]
    lax.fori_loop(SECOND_SPLIT, 2 * NH, mixing_unit, 0)
    swap = swap_half(1, 4, False, wait2)

    for n, h in enumerate(own_heads):
        cols, to = rows(h, HEAD_DIM), pl.ds(n * HEAD_DIM, HEAD_DIM)
        for b in range(2):
            both = pl.ds(b * BLK, BLK)
            after = after_ref[b, cols, :]
            kg_ref[both, to] = (dot_nt(v[both, cols], after) + kga[both, cols]).astype(BF16)
            vg_ref[both, to] = (dot_nn(k[both, cols], after) + vga[both, cols]).astype(BF16)
    wait_y = remote(gy.at[pl.ds(0, 2 * YS - 1)], gy.at[pl.ds(0, 2 * YS - 1)], 9, sibling)
    wait_y.wait_recv()
    gg_ref[...] = jnp.sum(gy[...], axis=0)[:NH]
    give.wait_send()
    wait1.wait_send()
    wait2.wait_send()
    wait_z.wait_send()
    wait_y.wait_send()
    for x in sends[0] + sends[1]:
        x.wait_send()
    swap.wait_recv()
    round_half(1, other, False)
    swap.wait_send()


def deliver(
    qg, kg, vg, gg, k, v, kga, vga, after_ref,
    qg_hbm, kg_hbm, vg_hbm, gg_hbm,
    kgo, vgo, sem,
):
    core = lax.axis_index("seq") % 2
    own = pl.ds(pl.multiple_of(core * HALF, HALF), HALF)
    other = pl.ds(pl.multiple_of((1 - core) * HALF, HALF), HALF)
    copies = []

    def send(src, dst):
        copies.append(pltpu.make_async_copy(src, dst, sem.at[len(copies)]))
        copies[-1].start()

    send(qg, qg_hbm)
    send(kg, kg_hbm.at[:, own])
    send(vg, vg_hbm.at[:, own])
    send(gg, gg_hbm)
    for b in range(2):
        both = pl.ds(b * BLK, BLK)
        for n in range(2):
            cols = pl.ds(pl.multiple_of((2 - 2 * core + n) * HEAD_DIM, HEAD_DIM), HEAD_DIM)
            to = pl.ds(n * HEAD_DIM, HEAD_DIM)
            after = after_ref[b, cols, :]
            kgo[both, to] = (dot_nt(v[both, cols], after) + kga[both, cols]).astype(BF16)
            vgo[both, to] = (dot_nn(k[both, cols], after) + vga[both, cols]).astype(BF16)
        send(kgo.at[both], kg_hbm.at[both, other])
        send(vgo.at[both], vg_hbm.at[both, other])
    for copy in copies:
        copy.wait()


def local(queries, keys, values, out_grad, gain):
    vmem = pltpu.VMEM
    big = jax.ShapeDtypeStruct((TOK, FEAT), BF16)
    state = (2, NH * HEAD_DIM, HEAD_DIM)
    half = (2, HALF, HEAD_DIM)
    tile = (8, HEAD_DIM)
    outside = pl.BlockSpec(memory_space=pltpu.HBM)
    whole = pl.BlockSpec(memory_space=vmem)
    results = (big, big, big, jax.ShapeDtypeStruct((NH, HEAD_DIM), F32))
    part = vmem((TOK, HALF), BF16)
    entire = vmem((TOK, FEAT), BF16)
    wide = vmem((TOK, FEAT), F32)
    kept = (
        entire, part, part, vmem((NH, HEAD_DIM), F32), entire, entire, wide, wide, vmem(state, BF16)
    )
    out = pl.pallas_call(
        kernel,
        name="attention_backward",
        out_shape=kept,
        in_specs=[outside] * 5,
        out_specs=(whole,) * len(kept),
        scratch_shapes=[
            vmem((TOK, FEAT), BF16),
            vmem((TOK, FEAT), BF16),
            vmem((1, FEAT), F32),
            vmem((2 * NH, BLK, BLK), BF16),
            vmem((TOK, FEAT), F32),
            vmem((TOK, FEAT), F32),
            vmem((TOK, FEAT), BF16),
            vmem((TOK, HEAD_DIM), F32),
            vmem((TOK, HEAD_DIM), F32),
            vmem(state, F32),
            vmem(state, F32),
            vmem(half, F32),
            vmem(half, F32),
            vmem(half, F32),
            vmem(half, F32),
            vmem(half, F32),
            vmem(half, F32),
            vmem(state, F32),
            vmem(state, BF16),
            vmem((2,) + tile, F32),
            vmem((3, 2) + tile, F32),
            vmem((2,) + tile, F32),
            vmem(tile, F32),
            vmem((ZS, 8, HEAD_DIM), F32),
            vmem(tile, F32),
            vmem((2 * YS, 8, HEAD_DIM), F32),
            pltpu.SemaphoreType.DMA((5,)),
            pltpu.SemaphoreType.DMA((17,)),
            pltpu.SemaphoreType.DMA((17,)),
        ],
        compiler_params=pltpu.CompilerParams(
            collective_id=0, has_side_effects=True, vmem_limit_bytes=40 * 1024 * 1024
        ),
    )(*(
        pltpu.with_memory_space_constraint(x, pltpu.HBM)
        for x in (queries, keys, values, out_grad, gain.reshape(1, FEAT))
    ))
    out = pl.pallas_call(
        deliver,
        name="deliver",
        out_shape=results,
        in_specs=[whole] * len(kept),
        out_specs=(outside,) * 4,
        scratch_shapes=[part, part, pltpu.SemaphoreType.DMA((8,))],
        compiler_params=pltpu.CompilerParams(vmem_limit_bytes=20 * 1024 * 1024),
    )(*out)
    return out[0], out[1], out[2], out[3].reshape(FEAT)


def solution(mesh):
    in_specs = (P("seq", "tp"), P("seq", "tp"), P("seq", "tp"), P("seq", "tp"), P("tp"))
    out_specs = (P("seq", "tp"), P("seq", "tp"), P("seq", "tp"), P("tp"))
    return jax.shard_map(local, mesh=mesh, in_specs=in_specs, out_specs=out_specs, check_vma=False)
```

```python
import jax
import jax.numpy as jnp
from jax import lax
from jax.experimental import pallas as pl
from jax.experimental.pallas import tpu as pltpu
from jax.sharding import PartitionSpec as P

HEAD_DIM = 128
BLK = 512
HALF = 256
NH = 4
TOK = 1024
FEAT = 512
FULL = 2048.0
YS = 4
ZS = 8
CHIPS = YS * ZS
PIECE = 8
EPS = 1e-05
MESH = pl.DeviceIdType.MESH
F32 = jnp.float32
BF16 = jnp.bfloat16

FIRST_SPLIT = 5
SECOND_SPLIT = 4


def ring(n, d):
    return min(d, n - d)


OFFSETS = sorted(
    [(dy, dz) for dy in range(YS) for dz in range(ZS) if (dy, dz) != (0, 0)],
    key=lambda o: -(ring(YS, o[0]) + ring(ZS, o[1])),
)


def dot_nn(a, b):
    return lax.dot_general(a, b, (((1,), (0,)), ((), ())), preferred_element_type=F32)


def dot_nt(a, b):
    return lax.dot_general(a, b, (((1,), (1,)), ((), ())), preferred_element_type=F32)


def dot_tn(a, b):
    return lax.dot_general(a, b, (((0,), (0,)), ((), ())), preferred_element_type=F32)


def kernel(
    q_hbm, k_hbm, v_hbm, g_hbm, gain_hbm,
    qg_ref, kg_ref, vg_ref, gg_ref, k, v, kga, vga, after_ref,
    q, g, gain, sc, att, scaled, da, rcol, mcol,
    inside, total, sib, piece, rb1, ob1, rb2, xb, edge, pref,
    tpo, tpr, coef, gchip, gz, gzs, gy,
    load_sem, send_sem, recv_sem,
):
    me = lax.axis_index("seq")
    tp = lax.axis_index("tp")
    chip = me // 2
    core = me % 2
    yy = chip // ZS
    zz = chip % ZS
    sibling = (me + 1 - 2 * core, tp)

    def chip_at(dy, dz):
        return (yy + dy) % YS * ZS + (zz + dz) % ZS

    turn = 1 - 2 * core
    chips = [chip_at(YS + turn * dy, ZS + turn * dz) for dy, dz in OFFSETS]
    crossed = [(2 * chip_at(dy, 0) + 1 - core, tp) for dy in (2, 1, 3)]
    tps = [(me, (tp + d) % 4) for d in (2, 1, 3)]

    barrier = pltpu.get_barrier_semaphore()
    peers = [(2 * c + core, tp) for c in chips] + crossed + tps + [sibling]
    for p in peers:
        pl.semaphore_signal(barrier, inc=1, device_id=p, device_id_type=MESH)

    loads = [
        pltpu.make_async_copy(src, dst, load_sem.at[i])
        for i, (src, dst) in enumerate(
            ((k_hbm, k), (v_hbm, v), (q_hbm, q), (g_hbm, g), (gain_hbm, gain))
        )
    ]
    loads[0].start()
    loads[1].start()

    def remote(src, dst, index, device):
        return pltpu.make_async_remote_copy(
            src_ref=src, dst_ref=dst, send_sem=send_sem.at[index], recv_sem=recv_sem.at[index],
            device_id=device, device_id_type=MESH,
        )

    def rows(i, n):
        return pl.ds(pl.multiple_of(i * n, n), n)

    row_id = lax.broadcasted_iota(jnp.int32, (HALF, HALF), 0)
    col_id = lax.broadcasted_iota(jnp.int32, (HALF, HALF), 1)
    causal = col_id <= row_id
    eye = (
        lax.broadcasted_iota(jnp.int32, (HEAD_DIM, HEAD_DIM), 0)
        == lax.broadcasted_iota(jnp.int32, (HEAD_DIM, HEAD_DIM), 1)
    )
    mine = rows(core, HALF)
    other = rows(1 - core, HALF)
    own_heads = [2 * core, 2 * core + 1]
    other_heads = [2 - 2 * core, 3 - 2 * core]

    def where_at(u):
        b = u // NH
        h = u % NH
        start = pl.multiple_of(b * BLK, BLK)
        return b, h, start, rows(h, HEAD_DIM)

    def states(heads, left, right, scan, inner):
        for h in heads:
            cols = rows(h, HEAD_DIM)
            first = dot_tn(left[pl.ds(0, BLK), cols], right[pl.ds(0, BLK), cols])
            second = dot_tn(left[pl.ds(BLK, BLK), cols], right[pl.ds(BLK, BLK), cols])
            inside[scan, cols, :] = second if inner == 1 else first
            total[scan, cols, :] = first + second

    def score_unit(u, carry):
        b, h, start, cols = where_at(u)
        upper, lower, both = pl.ds(start, HALF), pl.ds(start + HALF, HALF), pl.ds(start, BLK)
        top = jnp.where(causal, dot_nt(q[upper, cols], k[upper, cols]), 0.0).astype(BF16)
        low = dot_nt(q[lower, cols], k[upper, cols]).astype(BF16)
        end = jnp.where(causal, dot_nt(q[lower, cols], k[lower, cols]), 0.0).astype(BF16)
        sc[u, pl.ds(0, HALF), pl.ds(0, HALF)] = top
        sc[u, pl.ds(HALF, HALF), pl.ds(0, HALF)] = low
        sc[u, pl.ds(HALF, HALF), pl.ds(HALF, HALF)] = end
        att[upper, cols] = dot_nn(top, v[upper, cols])
        att[lower, cols] = dot_nn(low, v[upper, cols]) + dot_nn(end, v[lower, cols])
        scaled[both, cols] = gain[:, cols] * g[both, cols].astype(F32)
        return carry

    def mixing_unit(u, carry):
        b, h, start, cols = where_at(u)
        upper, lower, both = pl.ds(start, HALF), pl.ds(start + HALF, HALF), pl.ds(start, BLK)
        d_up, d_low = da[upper, cols], da[lower, cols]
        top = jnp.where(causal, dot_nt(d_up, v[upper, cols]), 0.0).astype(BF16)
        low = dot_nt(d_low, v[upper, cols]).astype(BF16)
        end = jnp.where(causal, dot_nt(d_low, v[lower, cols]), 0.0).astype(BF16)
        before = pref[b, cols, :]
        k_up, k_low = k[upper, cols], k[lower, cols]
        qg_ref[upper, cols] = (dot_nt(d_up, before) + dot_nn(top, k_up)).astype(BF16)
        qg_ref[lower, cols] = (
            dot_nt(d_low, before) + dot_nn(low, k_up) + dot_nn(end, k_low)
        ).astype(BF16)
        q_up, q_low = q[upper, cols], q[lower, cols]
        kga[upper, cols] = dot_tn(top, q_up) + dot_tn(low, q_low)
        kga[lower, cols] = dot_tn(end, q_low)
        s_top = sc[u, pl.ds(0, HALF), pl.ds(0, HALF)]
        s_low = sc[u, pl.ds(HALF, HALF), pl.ds(0, HALF)]
        s_end = sc[u, pl.ds(HALF, HALF), pl.ds(HALF, HALF)]
        vga[upper, cols] = dot_tn(s_top, d_up) + dot_tn(s_low, d_low)
        vga[lower, cols] = dot_tn(s_end, d_low)
        return carry

    nothing = (CHIPS - 1) * PIECE

    def give_half(scan, base):
        give = remote(total.at[scan, other], sib.at[scan], base, sibling)
        give.start()
        return give

    def spread(scan, base, give):
        give.wait_recv()
        piece[scan] = total[scan, mine, :] + sib[scan]
        for c in chips:
            remote(
                piece.at[scan, rows(c, PIECE)], rb1.at[scan, rows(chip, PIECE)], base + 1, (2 * c + core, tp)
            ).start()
        rb1[scan, rows(chip, PIECE), :] = piece[scan, rows(chip, PIECE), :]
        return remote(piece.at[scan, pl.ds(0, nothing)], rb1.at[scan, pl.ds(0, nothing)], base + 1, sibling)

    def scan_back(scan, base, forward, wait1):
        wait1.wait_recv()
        running = jnp.zeros((PIECE, HEAD_DIM), F32)
        for i in range(CHIPS):
            at = pl.ds((i if forward else CHIPS - 1 - i) * PIECE, PIECE)
            ob1[scan, at, :] = running
            running = running + rb1[scan, at, :]
        for c in chips:
            remote(
                ob1.at[scan, rows(c, PIECE)], rb2.at[scan, rows(chip, PIECE)], base + 2, (2 * c + core, tp)
            ).start()
        rb2[scan, rows(chip, PIECE), :] = ob1[scan, rows(chip, PIECE), :]
        return remote(ob1.at[scan, pl.ds(0, nothing)], rb2.at[scan, pl.ds(0, nothing)], base + 2, sibling)

    def round_half(scan, half, forward):
        reach = edge[scan, half, :]
        further = (reach + inside[scan, half, :]).astype(BF16)
        into = pref if forward else after_ref
        into[0 if forward else 1, half, :] = reach.astype(BF16)
        into[1 if forward else 0, half, :] = further

    def swap_half(scan, base, forward, wait2):
        wait2.wait_recv()
        late = core == 1 if forward else core == 0
        arrived = rb2[scan]
        xb[scan] = arrived + jnp.where(late, 0.0, total[scan, mine, :])
        swap = remote(xb.at[scan], edge.at[scan, mine], base + 3, sibling)
        swap.start()
        edge[scan, mine, :] = arrived + jnp.where(late, sib[scan], 0.0)
        round_half(scan, mine, forward)
        return swap

    loads[0].wait()
    loads[1].wait()
    for load in loads[2:]:
        load.start()
    states(other_heads, k, v, 0, 0)
    pl.semaphore_wait(barrier, len(peers))
    give = give_half(0, 0)
    states(own_heads, k, v, 0, 0)
    loads[2].wait()
    loads[3].wait()
    loads[4].wait()
    wait1 = spread(0, 0, give)
    lax.fori_loop(0, FIRST_SPLIT, score_unit, 0)
    wait2 = scan_back(0, 0, True, wait1)
    lax.fori_loop(FIRST_SPLIT, 2 * NH, score_unit, 0)
    swap = swap_half(0, 0, True, wait2)

    groups = BLK // HEAD_DIM

    def attend(heads, second, b):
        def body(j, carry):
            here = rows(b * groups + j, HEAD_DIM)
            squares, inner = (rcol[here], mcol[here]) if second else (0.0, 0.0)
            for h in heads:
                cols = rows(h, HEAD_DIM)
                a = att[here, cols] + dot_nn(q[here, cols], pref[b, cols, :])
                att[here, cols] = a
                squares = squares + a * a
                inner = inner + scaled[here, cols] * a
            if second:
                sq = jnp.sum(squares, axis=1, keepdims=True)
                inn = jnp.sum(inner, axis=1, keepdims=True)
                tpo[b, pl.ds(j, 1), :] = jnp.sum(jnp.where(eye, sq, 0.0), axis=0, keepdims=True)
                tpo[b, pl.ds(j + groups, 1), :] = jnp.sum(
                    jnp.where(eye, inn, 0.0), axis=0, keepdims=True
                )
            else:
                rcol[here] = squares
                mcol[here] = inner
            return carry

        lax.fori_loop(0, groups, body, 0, unroll=True)

    attend(own_heads, False, 0)
    attend(own_heads, False, 1)
    swap.wait_recv()
    round_half(0, other, True)
    sends = []
    for b in range(2):
        attend(other_heads, True, b)
        sends.append([remote(tpo.at[b], tpr.at[i, b], 11 + 3 * b + i, t) for i, t in enumerate(tps)])
        for x in sends[b]:
            x.start()
    give.wait_send()
    wait1.wait_send()
    wait2.wait_send()
    swap.wait_send()

    def grads(heads, second, b):
        def body(j, carry):
            here = rows(b * groups + j, HEAD_DIM)
            if second:
                r, m = rcol[here], mcol[here]
            else:
                r = jnp.sum(jnp.where(eye, coef[b, pl.ds(j, 1), :], 0.0), axis=1, keepdims=True)
                m = jnp.sum(
                    jnp.where(eye, coef[b, pl.ds(j + groups, 1), :], 0.0), axis=1, keepdims=True
                )
                r = jnp.broadcast_to(r, (HEAD_DIM, HEAD_DIM))
                m = jnp.broadcast_to(m, (HEAD_DIM, HEAD_DIM))
                rcol[here] = r
                mcol[here] = m
            for h in heads:
                cols = rows(h, HEAD_DIM)
                da[here, cols] = (r * scaled[here, cols] - m * att[here, cols]).astype(BF16)
            return carry

        lax.fori_loop(0, groups, body, 0, unroll=True)

    for b in range(2):
        for x in sends[b]:
            x.wait_recv()
        sums = tpo[b] + tpr[0, b] + tpr[1, b] + tpr[2, b]
        inverse = lax.rsqrt(sums[:groups] / FULL + EPS)
        coef[b, pl.ds(0, groups), :] = inverse
        coef[b, pl.ds(groups, groups), :] = inverse * inverse * inverse * (sums[groups:] / FULL)
        grads(other_heads, False, b)
    states(other_heads, q, da, 1, 1)
    give = give_half(1, 4)
    grads(own_heads, True, 0)
    grads(own_heads, True, 1)
    states(own_heads, q, da, 1, 1)
    wait1 = spread(1, 4, give)

    def gains(i, carry):
        here = rows(i, HEAD_DIM)
        r = rcol[here]
        sums = []
        for h in range(NH):
            cols = pl.ds(h * HEAD_DIM, HEAD_DIM)
            term = g[here, cols].astype(F32) * att[here, cols] * r
            sums.append(carry[h] + jnp.sum(term.reshape(HEAD_DIM // 8, 8, HEAD_DIM), axis=0))
        return tuple(sums)

    zero = jnp.zeros((8, HEAD_DIM), F32)
    parts = lax.fori_loop(0, TOK // HEAD_DIM, gains, (zero,) * NH)
    for h in range(NH):
        gchip[pl.ds(h, 1), :] = jnp.sum(parts[h], axis=0, keepdims=True)
    for d in (4, 3, 5, 2, 6, 1, 7):
        c = chip_at(0, d)
        remote(gchip, gz.at[zz], 8, (2 * c + core, tp)).start()
    gz[zz] = gchip[...]
    lax.fori_loop(0, SECOND_SPLIT, mixing_unit, 0)
    wait2 = scan_back(1, 4, False, wait1)
    wait_z = remote(gz.at[pl.ds(0, ZS - 1)], gz.at[pl.ds(0, ZS - 1)], 8, sibling)
    wait_z.wait_recv()
    gzs[...] = jnp.sum(gz[...], axis=0)
    for p in crossed + [(2 * chip_at(d, 0) + core, tp) for d in (2, 1, 3)] + [sibling]:
        remote(gzs, gy.at[2 * yy + core], 9, p).start()
    gy[2 * yy + core] = gzs[...]
    lax.fori_loop(SECOND_SPLIT, 2 * NH, mixing_unit, 0)
    swap = swap_half(1, 4, False, wait2)

    for n, h in enumerate(own_heads):
        cols, to = rows(h, HEAD_DIM), pl.ds(n * HEAD_DIM, HEAD_DIM)
        for b in range(2):
            both = pl.ds(b * BLK, BLK)
            after = after_ref[b, cols, :]
            kg_ref[both, to] = (dot_nt(v[both, cols], after) + kga[both, cols]).astype(BF16)
            vg_ref[both, to] = (dot_nn(k[both, cols], after) + vga[both, cols]).astype(BF16)
    wait_y = remote(gy.at[pl.ds(0, 2 * YS - 1)], gy.at[pl.ds(0, 2 * YS - 1)], 9, sibling)
    wait_y.wait_recv()
    gg_ref[...] = jnp.sum(gy[...], axis=0)
    give.wait_send()
    wait1.wait_send()
    wait2.wait_send()
    wait_z.wait_send()
    wait_y.wait_send()
    for x in sends[0] + sends[1]:
        x.wait_send()
    swap.wait_recv()
    round_half(1, other, False)
    swap.wait_send()


def deliver(
    qg, kg, vg, gg, k, v, kga, vga, after_ref,
    qg_hbm, kg_hbm, vg_hbm, gg_hbm,
    kgo, vgo, sem,
):
    core = lax.axis_index("seq") % 2
    own = pl.ds(pl.multiple_of(core * HALF, HALF), HALF)
    other = pl.ds(pl.multiple_of((1 - core) * HALF, HALF), HALF)
    copies = []

    def send(src, dst):
        copies.append(pltpu.make_async_copy(src, dst, sem.at[len(copies)]))
        copies[-1].start()

    send(qg, qg_hbm)
    send(kg, kg_hbm.at[:, own])
    send(vg, vg_hbm.at[:, own])
    send(gg, gg_hbm)
    for b in range(2):
        both = pl.ds(b * BLK, BLK)
        for n in range(2):
            cols = pl.ds(pl.multiple_of((2 - 2 * core + n) * HEAD_DIM, HEAD_DIM), HEAD_DIM)
            to = pl.ds(n * HEAD_DIM, HEAD_DIM)
            after = after_ref[b, cols, :]
            kgo[both, to] = (dot_nt(v[both, cols], after) + kga[both, cols]).astype(BF16)
            vgo[both, to] = (dot_nn(k[both, cols], after) + vga[both, cols]).astype(BF16)
        send(kgo.at[both], kg_hbm.at[both, other])
        send(vgo.at[both], vg_hbm.at[both, other])
    for copy in copies:
        copy.wait()


def local(queries, keys, values, out_grad, gain):
    vmem = pltpu.VMEM
    big = jax.ShapeDtypeStruct((TOK, FEAT), BF16)
    state = (2, NH * HEAD_DIM, HEAD_DIM)
    half = (2, HALF, HEAD_DIM)
    tile = (8, HEAD_DIM)
    outside = pl.BlockSpec(memory_space=pltpu.HBM)
    whole = pl.BlockSpec(memory_space=vmem)
    results = (big, big, big, jax.ShapeDtypeStruct((NH, HEAD_DIM), F32))
    part = vmem((TOK, HALF), BF16)
    entire = vmem((TOK, FEAT), BF16)
    wide = vmem((TOK, FEAT), F32)
    kept = (
        entire, part, part, vmem((NH, HEAD_DIM), F32), entire, entire, wide, wide, vmem(state, BF16)
    )
    out = pl.pallas_call(
        kernel,
        name="attention_backward",
        out_shape=kept,
        in_specs=[outside] * 5,
        out_specs=(whole,) * len(kept),
        scratch_shapes=[
            vmem((TOK, FEAT), BF16),
            vmem((TOK, FEAT), BF16),
            vmem((1, FEAT), F32),
            vmem((2 * NH, BLK, BLK), BF16),
            vmem((TOK, FEAT), F32),
            vmem((TOK, FEAT), F32),
            vmem((TOK, FEAT), BF16),
            vmem((TOK, HEAD_DIM), F32),
            vmem((TOK, HEAD_DIM), F32),
            vmem(state, F32),
            vmem(state, F32),
            vmem(half, F32),
            vmem(half, F32),
            vmem(half, F32),
            vmem(half, F32),
            vmem(half, F32),
            vmem(half, F32),
            vmem(state, F32),
            vmem(state, BF16),
            vmem((2,) + tile, F32),
            vmem((3, 2) + tile, F32),
            vmem((2,) + tile, F32),
            vmem((NH, HEAD_DIM), F32),
            vmem((ZS, NH, HEAD_DIM), F32),
            vmem((NH, HEAD_DIM), F32),
            vmem((2 * YS, NH, HEAD_DIM), F32),
            pltpu.SemaphoreType.DMA((5,)),
            pltpu.SemaphoreType.DMA((17,)),
            pltpu.SemaphoreType.DMA((17,)),
        ],
        compiler_params=pltpu.CompilerParams(
            collective_id=0, has_side_effects=True, vmem_limit_bytes=40 * 1024 * 1024
        ),
    )(*(
        pltpu.with_memory_space_constraint(x, pltpu.HBM)
        for x in (queries, keys, values, out_grad, gain.reshape(1, FEAT))
    ))
    out = pl.pallas_call(
        deliver,
        name="deliver",
        out_shape=results,
        in_specs=[whole] * len(kept),
        out_specs=(outside,) * 4,
        scratch_shapes=[part, part, pltpu.SemaphoreType.DMA((8,))],
        compiler_params=pltpu.CompilerParams(vmem_limit_bytes=20 * 1024 * 1024),
    )(*out)
    return out[0], out[1], out[2], out[3].reshape(FEAT)


def solution(mesh):
    in_specs = (P("seq", "tp"), P("seq", "tp"), P("seq", "tp"), P("seq", "tp"), P("tp"))
    out_specs = (P("seq", "tp"), P("seq", "tp"), P("seq", "tp"), P("tp"))
    return jax.shard_map(local, mesh=mesh, in_specs=in_specs, out_specs=out_specs, check_vma=False)
```
